32 devices in a mesh: group: 2 (over core), blk: 16 (over z, y, x).
Axes of the slice: x: 2, y: 2, z: 4, core: 2. Of those that a mesh axis runs over, the one named last changes fastest.
Arguments:
- picture_vectors: bfloat16 [4096, 1152], P(('group', 'blk')), may hold values from -1 to 1
- caption_vectors: bfloat16 [4096, 1152], P(('group', 'blk')), may hold values from -1 to 1
- inverse_heat_factor: float32 [1], replicated, may hold values from 0.5 to 2
- score_shift_term: float32 [1], replicated, may hold values from -3 to 1
Outputs:
- grad_images: float32 [4096, 1152], P(('group', 'blk'))
- grad_texts: float32 [4096, 1152], P(('group', 'blk'))
- row_loss: float32 [4096], P(('group', 'blk'))
The draws below stay inside these ranges and needn't reach their ends.
All inputs are finite; a program needn't handle non-finite values.
Results may differ from the reference program's by a relative error of at most 0.015.
Values may be sent and summed in bfloat16 or wider, within the bound.
A program may use at most 64 MiB of HBM per device.

```python
import math
import jax
import jax.numpy as jnp
from jax import lax

D = 1152
ROWS = 128
SPAN = 2
BUNDLE = 256
TOKENS = 4096
N_GROUP = 2
N_BLK = 16


def block_scale(stream_key, extent, pieces, least, top_value):
    factor_of, own = 1.0, jax.random.fold_in(stream_key, 6)
    for position, parts in pieces:
        heights = jnp.exp(jax.random.uniform(jax.random.fold_in(own, position), (parts,), jnp.float32, least / len(pieces), top_value / len(pieces)))
        factor_of = factor_of * jnp.repeat(heights, extent[position] // parts).reshape([-1 if axis == position else 1 for axis in range(len(extent))])
    return factor_of


def centred(key, dims, width, bound, cuts=(), dtype=jnp.bfloat16):
    values = width * jax.random.normal(key, dims, jnp.float32)
    if cuts:
        values = values * block_scale(key, dims, cuts, -0.22, 0.18)
    return jnp.clip(values, -bound, bound).astype(dtype)


def setup_inputs(seed: int = 0) -> dict:
    splits = jax.random.split(jax.random.key(seed), 5)
    picture_vectors = centred(splits[0], (TOKENS, D), 0.171, 1.0, ((0, 32),))
    caption_vectors = centred(splits[1], (TOKENS, D), 0.171, 1.0, ((0, 32),))
    inverse_heat_factor = jnp.clip(jnp.exp(jax.random.uniform(splits[2], (1,), jnp.float32, math.log(0.5), math.log(2.0))), 0.5, 2.0)
    score_shift_term = jnp.clip(jax.random.uniform(splits[3], (1,), jnp.float32, -3.0, 1.0), -3.0, 1.0)
    return {"picture_vectors": picture_vectors, "caption_vectors": caption_vectors, "inverse_heat_factor": inverse_heat_factor, "score_shift_term": score_shift_term}


def reference(picture_vectors, caption_vectors, inverse_heat_factor, score_shift_term):
    group_width = N_GROUP
    cycle_size = N_BLK
    image_four = picture_vectors.reshape(group_width, cycle_size, ROWS, D).astype(jnp.float32)
    text_quad_block = caption_vectors.reshape(group_width, cycle_size, ROWS, D)
    score_multiplier = inverse_heat_factor[0]
    shift_value = score_shift_term[0]
    bundles = []
    for step in range(SPAN):
        rolled = jnp.roll(text_quad_block, step, axis=1)
        bundles.append(rolled.transpose(1, 0, 2, 3).reshape(cycle_size, BUNDLE, D).astype(jnp.float32))
    loss_rows = []
    image_rows = []
    text_total = jnp.zeros((cycle_size, BUNDLE, D), jnp.float32)
    for group_id in range(group_width):
        images_here = image_four[group_id]
        positives = jnp.arange(BUNDLE)[None, :] == (group_id * ROWS + jnp.arange(ROWS)[:, None])
        positives = positives[None, :, :]
        loss_sum = jnp.zeros((cycle_size, ROWS), jnp.float32)
        grad_image = jnp.zeros((cycle_size, ROWS, D), jnp.float32)
        group_part = jnp.zeros((cycle_size, BUNDLE, D), jnp.float32)
        for step in range(SPAN):
            text_bundle = bundles[step]
            logits = jnp.einsum("brd,bhd->brh", images_here, text_bundle)
            scaled = score_multiplier * logits + shift_value
            if step == 0:
                signs = jnp.where(positives, 1.0, -1.0).astype(jnp.float32) * jnp.ones_like(scaled)
            else:
                signs = -jnp.ones_like(scaled)
            loss_sum = loss_sum + jnp.sum(jax.nn.softplus(-signs * scaled), axis=-1)
            slopes = (-signs * jax.nn.sigmoid(-signs * scaled) * score_multiplier).astype(jnp.bfloat16).astype(jnp.float32)
            grad_image = grad_image + jnp.einsum("brh,bhd->brd", slopes, text_bundle)
            grad_bundle = jnp.einsum("brh,brd->bhd", slopes, images_here)
            group_part = group_part + jnp.roll(grad_bundle, -step, axis=0)
        rounded = lax.optimization_barrier(group_part.astype(jnp.bfloat16))
        text_total = text_total + rounded.astype(jnp.float32)
        loss_rows.append(loss_sum)
        image_rows.append(grad_image)
    grad_text = text_total.reshape(cycle_size, group_width, ROWS, D).transpose(1, 0, 2, 3)
    loss_all = jnp.stack(loss_rows, axis=0)
    grad_image_all = jnp.stack(image_rows, axis=0)
    row_loss = (loss_all / (SPAN * BUNDLE)).reshape(TOKENS)
    return grad_image_all.reshape(TOKENS, D), grad_text.reshape(TOKENS, D), row_loss
```

```python
import functools

import jax
import jax.numpy as jnp
from jax import lax
from jax.experimental import pallas as pl
from jax.experimental.pallas import tpu as pltpu
from jax.sharding import PartitionSpec as P

SPAN = 2
PIECES = 4
TEXT, IMAGE = 0, 1


def kernel(
    group_width, cycle, images, texts, scale, shift, grad_images, grad_texts, row_loss,
    near, far, load_sem, near_send, near_recv, far_send, far_recv, pass_send, pass_recv,
):
    group, place = lax.axis_index("group"), lax.axis_index("blk")
    after, before = lax.rem(place + 1, cycle), lax.rem(place + cycle - 1, cycle)
    rows = images.shape[0]
    piece = rows // PIECES
    sources = (texts, images)
    onward = (after, before)

    def peer(k):
        return lax.rem(group + k, group_width)

    def over_peers(body):
        if group_width <= 2:
            for k in range(1, group_width):
                body(k)
        else:
            pl.loop(1, group_width)(body)

    def loads(kind):
        return pltpu.make_async_copy(sources[kind], near.at[kind, group], load_sem.at[kind])

    def near_copy(kind, k):
        return pltpu.make_async_remote_copy(
            src_ref=sources[kind], dst_ref=near.at[kind, group],
            send_sem=near_send.at[kind, k], recv_sem=near_recv.at[kind, k],
            device_id=(peer(k), place), device_id_type=pl.DeviceIdType.MESH,
        )

    def far_copy(kind, c):
        part = pl.ds(c * piece, piece)
        return pltpu.make_async_remote_copy(
            src_ref=sources[kind].at[part], dst_ref=far.at[kind, group, part],
            send_sem=far_send.at[kind, c], recv_sem=far_recv.at[kind, c],
            device_id=(group, onward[kind]), device_id_type=pl.DeviceIdType.MESH,
        )

    def pass_copy(kind, c, k):
        block = far.at[kind, group, pl.ds(c * piece, piece)]
        return pltpu.make_async_remote_copy(
            src_ref=block, dst_ref=block,
            send_sem=pass_send.at[kind, c, k], recv_sem=pass_recv.at[kind, c, k],
            device_id=(peer(k), place), device_id_type=pl.DeviceIdType.MESH,
        )

    def sender(k):
        return lax.rem(group + group_width - k, group_width)

    for kind in (TEXT, IMAGE):
        loads(kind).start()
    barrier = pltpu.get_barrier_semaphore()
    for neighbour in (after, before):
        pl.semaphore_signal(
            barrier, inc=1, device_id=(group, neighbour), device_id_type=pl.DeviceIdType.MESH
        )

    def greet(k):
        pl.semaphore_signal(
            barrier, inc=1, device_id=(peer(k), place), device_id_type=pl.DeviceIdType.MESH
        )

    over_peers(greet)
    pl.semaphore_wait(barrier, group_width + 1)

    for c in range(PIECES):
        for kind in (TEXT, IMAGE):
            far_copy(kind, c).start()
    for kind in (TEXT, IMAGE):
        over_peers(lambda k: near_copy(kind, k).start())

    factor, offset = scale[0], shift[0]
    outputs = (grad_images, grad_texts)

    def meet(kind, block, diagonal=False, first=False):
        own = near[1 - kind, group]
        z = lax.dot_general(
            block, own, (((1,), (1,)), ((), ())), preferred_element_type=jnp.float32
        )
        z = factor * z + offset
        if diagonal:
            same = lax.broadcasted_iota(jnp.int32, z.shape, 0) == lax.broadcasted_iota(
                jnp.int32, z.shape, 1
            )
            z = jnp.where(same, -z, z)
        small = jnp.exp(-jnp.abs(z))
        slopes = factor * (jnp.where(z >= 0, 1.0, small) / (1.0 + small))
        if diagonal:
            slopes = jnp.where(same, -slopes, slopes)
        if kind == TEXT:
            loss = jnp.sum(jnp.maximum(z, 0.0) + jnp.log1p(small), axis=0, keepdims=True)
            row_loss[...] = loss if first else row_loss[...] + loss
        grad = lax.dot_general(
            slopes.astype(jnp.bfloat16), block, (((0,), (0,)), ((), ())),
            preferred_element_type=jnp.float32,
        )
        out = outputs[kind]
        out[...] = grad if first else out[...] + grad

    for kind in (TEXT, IMAGE):
        loads(kind).wait()
    for kind in (TEXT, IMAGE):
        meet(kind, near[kind, group], diagonal=True, first=True)

    def meet_near(k):
        for kind in (TEXT, IMAGE):
            near_copy(kind, k).wait_recv()
            meet(kind, near[kind, sender(k)])

    over_peers(meet_near)

    def meet_passed(c):
        def one(k):
            for kind in (TEXT, IMAGE):
                pass_copy(kind, c, k).wait_recv()
                meet(kind, far[kind, sender(k), pl.ds(c * piece, piece)])

        over_peers(one)

    for c in range(PIECES):
        for kind in (TEXT, IMAGE):
            far_copy(kind, c).wait_recv()
            over_peers(lambda k: pass_copy(kind, c, k).start())
        if c > 0:
            meet_passed(c - 1)
        for kind in (TEXT, IMAGE):
            meet(kind, far[kind, group, pl.ds(c * piece, piece)])
    meet_passed(PIECES - 1)
    row_loss[...] = row_loss[...] / (SPAN * group_width * rows)

    for kind in (TEXT, IMAGE):
        for c in range(PIECES):
            far_copy(kind, c).wait_send()

    def sent(k):
        for kind in (TEXT, IMAGE):
            near_copy(kind, k).wait_send()
            for c in range(PIECES):
                pass_copy(kind, c, k).wait_send()

    over_peers(sent)


def shards(group_width, cycle, images, texts, scale, shift):
    rows, width = images.shape
    flops = 4 * 2 * rows * SPAN * group_width * rows * width
    grad_images, grad_texts, row_loss = pl.pallas_call(
        functools.partial(kernel, group_width, cycle),
        out_shape=(
            jax.ShapeDtypeStruct((rows, width), jnp.float32),
            jax.ShapeDtypeStruct((rows, width), jnp.float32),
            jax.ShapeDtypeStruct((1, rows), jnp.float32),
        ),
        in_specs=[pl.BlockSpec(memory_space=pl.ANY)] * 2
        + [pl.BlockSpec(memory_space=pltpu.SMEM)] * 2,
        out_specs=[pl.BlockSpec(memory_space=pltpu.VMEM)] * 3,
        scratch_shapes=[
            pltpu.VMEM((2, group_width, rows, width), images.dtype),
            pltpu.VMEM((2, group_width, rows, width), images.dtype),
            pltpu.SemaphoreType.DMA((2,)),
            pltpu.SemaphoreType.DMA((2, group_width)),
            pltpu.SemaphoreType.DMA((2, group_width)),
            pltpu.SemaphoreType.DMA((2, PIECES)),
            pltpu.SemaphoreType.DMA((2, PIECES)),
            pltpu.SemaphoreType.DMA((2, PIECES, group_width)),
            pltpu.SemaphoreType.DMA((2, PIECES, group_width)),
        ],
        compiler_params=pltpu.CompilerParams(
            collective_id=0, has_side_effects=True, vmem_limit_bytes=32 << 20
        ),
        cost_estimate=pl.CostEstimate(
            flops=flops, bytes_accessed=16 * rows * width, transcendentals=0
        ),
    )(images, texts, scale, shift)
    return grad_images, grad_texts, row_loss.reshape(rows)


def solution(mesh):
    placed = (P(("group", "blk"), None), P(("group", "blk"), None), P(), P())
    return jax.shard_map(
        functools.partial(shards, mesh.shape["group"], mesh.shape["blk"]),
        mesh=mesh,
        in_specs=placed,
        out_specs=(P(("group", "blk"), None), P(("group", "blk"), None), P(("group", "blk"))),
        check_vma=False,
    )
```

```python
import functools

import jax
import jax.numpy as jnp
from jax import lax
from jax.experimental import pallas as pl
from jax.experimental.pallas import tpu as pltpu
from jax.sharding import PartitionSpec as P

SPAN = 2
PIECES = 4
TEXT, IMAGE = 0, 1


def kernel(
    group_width, cycle, images, texts, scale, shift, grad_images, grad_texts, row_loss,
    near, far, load_sem, near_send, near_recv, far_send, far_recv, pass_send, pass_recv,
):
    group, place = lax.axis_index("group"), lax.axis_index("blk")
    after, before = lax.rem(place + 1, cycle), lax.rem(place + cycle - 1, cycle)
    rows = images.shape[0]
    piece = rows // PIECES
    sources = (texts, images)
    onward = (after, before)

    def peer(k):
        return lax.rem(group + k, group_width)

    def over_peers(body):
        if group_width <= 2:
            for k in range(1, group_width):
                body(k)
        else:
            pl.loop(1, group_width)(body)

    def loads(kind):
        return pltpu.make_async_copy(sources[kind], near.at[kind, group], load_sem.at[kind])

    def near_copy(kind, k):
        return pltpu.make_async_remote_copy(
            src_ref=sources[kind], dst_ref=near.at[kind, group],
            send_sem=near_send.at[kind, k], recv_sem=near_recv.at[kind, k],
            device_id=(peer(k), place), device_id_type=pl.DeviceIdType.MESH,
        )

    def far_copy(kind, c):
        part = pl.ds(c * piece, piece)
        return pltpu.make_async_remote_copy(
            src_ref=sources[kind].at[part], dst_ref=far.at[kind, group, part],
            send_sem=far_send.at[kind, c], recv_sem=far_recv.at[kind, c],
            device_id=(group, onward[kind]), device_id_type=pl.DeviceIdType.MESH,
        )

    def pass_copy(kind, c, k):
        block = far.at[kind, group, pl.ds(c * piece, piece)]
        return pltpu.make_async_remote_copy(
            src_ref=block, dst_ref=block,
            send_sem=pass_send.at[kind, c, k], recv_sem=pass_recv.at[kind, c, k],
            device_id=(peer(k), place), device_id_type=pl.DeviceIdType.MESH,
        )

    def sender(k):
        return lax.rem(group + group_width - k, group_width)

    for kind in (TEXT, IMAGE):
        loads(kind).start()
    barrier = pltpu.get_barrier_semaphore()
    for neighbour in (after, before):
        pl.semaphore_signal(
            barrier, inc=1, device_id=(group, neighbour), device_id_type=pl.DeviceIdType.MESH
        )

    def greet(k):
        pl.semaphore_signal(
            barrier, inc=1, device_id=(peer(k), place), device_id_type=pl.DeviceIdType.MESH
        )

    over_peers(greet)
    pl.semaphore_wait(barrier, group_width + 1)

    for c in range(PIECES):
        for kind in (TEXT, IMAGE):
            far_copy(kind, c).start()
    for kind in (TEXT, IMAGE):
        over_peers(lambda k: near_copy(kind, k).start())

    factor, offset = scale[0], shift[0]
    outputs = (grad_images, grad_texts)

    def meet(kind, block, diagonal=False, first=False):
        own = near[1 - kind, group]
        z = lax.dot_general(
            block, own, (((1,), (1,)), ((), ())), preferred_element_type=jnp.float32
        )
        z = factor * z + offset
        if diagonal:
            same = lax.broadcasted_iota(jnp.int32, z.shape, 0) == lax.broadcasted_iota(
                jnp.int32, z.shape, 1
            )
            z = jnp.where(same, -z, z)
        small = jnp.exp(-jnp.abs(z))
        slopes = factor * (jnp.where(z >= 0, 1.0, small) / (1.0 + small))
        if diagonal:
            slopes = jnp.where(same, -slopes, slopes)
        if kind == TEXT:
            loss = jnp.sum(jnp.maximum(z, 0.0) + jnp.log1p(small), axis=0, keepdims=True)
            row_loss[...] = loss if first else row_loss[...] + loss
        grad = lax.dot_general(
            slopes.astype(jnp.bfloat16), block, (((0,), (0,)), ((), ())),
            preferred_element_type=jnp.float32,
        )
        out = outputs[kind]
        out[...] = grad if first else out[...] + grad

    for kind in (TEXT, IMAGE):
        loads(kind).wait()
    for kind in (TEXT, IMAGE):
        meet(kind, near[kind, group], diagonal=True, first=True)

    def meet_near(k):
        for kind in (TEXT, IMAGE):
            near_copy(kind, k).wait_recv()
            meet(kind, near[kind, sender(k)])

    over_peers(meet_near)

    def meet_passed(c):
        def one(k):
            for kind in (TEXT, IMAGE):
                pass_copy(kind, c, k).wait_recv()
                meet(kind, far[kind, sender(k), pl.ds(c * piece, piece)])

        over_peers(one)

    for c in range(PIECES):
        for kind in (TEXT, IMAGE):
            far_copy(kind, c).wait_recv()
            over_peers(lambda k: pass_copy(kind, c, k).start())
        if c > 0:
            meet_passed(c - 1)
        for kind in (TEXT, IMAGE):
            meet(kind, far[kind, group, pl.ds(c * piece, piece)])
    meet_passed(PIECES - 1)
    row_loss[...] = row_loss[...] / (SPAN * group_width * rows)

    for kind in (TEXT, IMAGE):
        for c in range(PIECES):
            far_copy(kind, c).wait_send()

    def sent(k):
        for kind in (TEXT, IMAGE):
            near_copy(kind, k).wait_send()
            for c in range(PIECES):
                pass_copy(kind, c, k).wait_send()

    over_peers(sent)


def store(*refs):
    count = len(refs) // 2
    held, out, sem = refs[:count], refs[count:-1], refs[-1]
    copies = [pltpu.make_async_copy(a, b, sem.at[i]) for i, (a, b) in enumerate(zip(held, out))]
    for copy in copies:
        copy.start()
    for copy in copies:
        copy.wait()


def shards(group_width, cycle, images, texts, scale, shift):
    rows, width = images.shape
    flops = 4 * 2 * rows * SPAN * group_width * rows * width
    shapes = (
        jax.ShapeDtypeStruct((rows, width), jnp.float32),
        jax.ShapeDtypeStruct((rows, width), jnp.float32),
        jax.ShapeDtypeStruct((1, rows), jnp.float32),
    )
    results = pl.pallas_call(
        functools.partial(kernel, group_width, cycle),
        out_shape=shapes,
        in_specs=[pl.BlockSpec(memory_space=pltpu.HBM)] * 2
        + [pl.BlockSpec(memory_space=pltpu.SMEM)] * 2,
        out_specs=[pl.BlockSpec(memory_space=pltpu.VMEM)] * 3,
        scratch_shapes=[
            pltpu.VMEM((2, group_width, rows, width), images.dtype),
            pltpu.VMEM((2, group_width, rows, width), images.dtype),
            pltpu.SemaphoreType.DMA((2,)),
            pltpu.SemaphoreType.DMA((2, group_width)),
            pltpu.SemaphoreType.DMA((2, group_width)),
            pltpu.SemaphoreType.DMA((2, PIECES)),
            pltpu.SemaphoreType.DMA((2, PIECES)),
            pltpu.SemaphoreType.DMA((2, PIECES, group_width)),
            pltpu.SemaphoreType.DMA((2, PIECES, group_width)),
        ],
        compiler_params=pltpu.CompilerParams(
            collective_id=0, has_side_effects=True, vmem_limit_bytes=32 << 20
        ),
        cost_estimate=pl.CostEstimate(
            flops=flops, bytes_accessed=16 * rows * width, transcendentals=0
        ),
    )(
        pltpu.with_memory_space_constraint(images, pltpu.HBM),
        pltpu.with_memory_space_constraint(texts, pltpu.HBM),
        scale,
        shift,
    )
    grad_images, grad_texts, row_loss = pl.pallas_call(
        store,
        out_shape=shapes,
        in_specs=[pl.BlockSpec(memory_space=pltpu.VMEM)] * 3,
        out_specs=[pl.BlockSpec(memory_space=pltpu.HBM)] * 3,
        scratch_shapes=[pltpu.SemaphoreType.DMA((3,))],
        compiler_params=pltpu.CompilerParams(vmem_limit_bytes=8 << 20),
        cost_estimate=pl.CostEstimate(
            flops=0, bytes_accessed=16 * rows * width, transcendentals=0
        ),
    )(*results)
    return grad_images, grad_texts, row_loss.reshape(rows)


def solution(mesh):
    placed = (P(("group", "blk"), None), P(("group", "blk"), None), P(), P())
    return jax.shard_map(
        functools.partial(shards, mesh.shape["group"], mesh.shape["blk"]),
        mesh=mesh,
        in_specs=placed,
        out_specs=(P(("group", "blk"), None), P(("group", "blk"), None), P(("group", "blk"))),
        check_vma=False,
    )
```

```python
import functools

import jax
import jax.numpy as jnp
from jax import lax
from jax.experimental import pallas as pl
from jax.experimental.pallas import tpu as pltpu
from jax.sharding import PartitionSpec as P

SPAN = 2
PIECES = 4
TEXT, IMAGE = 0, 1


def kernel(
    group_width, cycle, images, texts, scale, shift, grad_images, grad_texts, row_loss,
    near, far, load_sem, near_send, near_recv, far_send, far_recv, pass_send, pass_recv,
):
    group, place = lax.axis_index("group"), lax.axis_index("blk")
    after, before = lax.rem(place + 1, cycle), lax.rem(place + cycle - 1, cycle)
    rows = images.shape[0]
    piece = rows // PIECES
    sources = (texts, images)
    onward = (after, before)

    def peer(k):
        return lax.rem(group + k, group_width)

    def over_peers(body):
        if group_width <= 2:
            for k in range(1, group_width):
                body(k)
        else:
            pl.loop(1, group_width)(body)

    def own(kind):
        return near.at[kind, pl.ds(pl.multiple_of(group * rows, rows), rows)]

    def own_piece(kind, c):
        return far.at[kind, c, pl.ds(pl.multiple_of(group * piece, piece), piece)]

    def loads(kind):
        return pltpu.make_async_copy(sources[kind], own(kind), load_sem.at[kind])

    def near_copy(kind, k):
        return pltpu.make_async_remote_copy(
            src_ref=sources[kind], dst_ref=own(kind),
            send_sem=near_send.at[kind, k], recv_sem=near_recv.at[kind, k],
            device_id=(peer(k), place), device_id_type=pl.DeviceIdType.MESH,
        )

    def far_copy(kind, c):
        return pltpu.make_async_remote_copy(
            src_ref=sources[kind].at[pl.ds(c * piece, piece)], dst_ref=own_piece(kind, c),
            send_sem=far_send.at[kind, c], recv_sem=far_recv.at[kind, c],
            device_id=(group, onward[kind]), device_id_type=pl.DeviceIdType.MESH,
        )

    def pass_copy(kind, c, k):
        return pltpu.make_async_remote_copy(
            src_ref=own_piece(kind, c), dst_ref=own_piece(kind, c),
            send_sem=pass_send.at[kind, c, k], recv_sem=pass_recv.at[kind, c, k],
            device_id=(peer(k), place), device_id_type=pl.DeviceIdType.MESH,
        )

    for kind in (TEXT, IMAGE):
        loads(kind).start()
    barrier = pltpu.get_barrier_semaphore()
    for neighbour in (after, before):
        pl.semaphore_signal(
            barrier, inc=1, device_id=(group, neighbour), device_id_type=pl.DeviceIdType.MESH
        )

    def greet(k):
        pl.semaphore_signal(
            barrier, inc=1, device_id=(peer(k), place), device_id_type=pl.DeviceIdType.MESH
        )

    over_peers(greet)
    pl.semaphore_wait(barrier, group_width + 1)

    for c in range(PIECES):
        for kind in (TEXT, IMAGE):
            far_copy(kind, c).start()
    for kind in (TEXT, IMAGE):
        over_peers(lambda k: near_copy(kind, k).start())

    factor, offset = scale[0], shift[0]
    outputs = (grad_images, grad_texts)

    def meet(kind, block, first=False):
        z = lax.dot_general(
            block, own(1 - kind)[...], (((1,), (1,)), ((), ())), preferred_element_type=jnp.float32
        )
        z = factor * z + offset
        if first:
            same = lax.broadcasted_iota(jnp.int32, z.shape, 0) == (
                lax.broadcasted_iota(jnp.int32, z.shape, 1) + group * rows
            )
            z = jnp.where(same, -z, z)
        small = jnp.exp(-jnp.abs(z))
        slopes = factor * (jnp.where(z >= 0, 1.0, small) / (1.0 + small))
        if first:
            slopes = jnp.where(same, -slopes, slopes)
        if kind == TEXT:
            loss = jnp.sum(jnp.maximum(z, 0.0) + jnp.log1p(small), axis=0, keepdims=True)
            row_loss[...] = loss if first else row_loss[...] + loss
        grad = lax.dot_general(
            slopes.astype(jnp.bfloat16), block, (((0,), (0,)), ((), ())),
            preferred_element_type=jnp.float32,
        )
        out = outputs[kind]
        out[...] = grad if first else out[...] + grad

    for kind in (TEXT, IMAGE):
        loads(kind).wait()
        over_peers(lambda k: near_copy(kind, k).wait_recv())
    for kind in (TEXT, IMAGE):
        meet(kind, near[kind], first=True)

    def meet_far(c):
        for kind in (TEXT, IMAGE):
            over_peers(lambda k: pass_copy(kind, c, k).wait_recv())
        for kind in (TEXT, IMAGE):
            meet(kind, far[kind, c])

    for c in range(PIECES):
        for kind in (TEXT, IMAGE):
            far_copy(kind, c).wait_recv()
            over_peers(lambda k: pass_copy(kind, c, k).start())
        if c > 0:
            meet_far(c - 1)
    meet_far(PIECES - 1)
    row_loss[...] = row_loss[...] / (SPAN * group_width * rows)

    for kind in (TEXT, IMAGE):
        for c in range(PIECES):
            far_copy(kind, c).wait_send()

    def sent(k):
        for kind in (TEXT, IMAGE):
            near_copy(kind, k).wait_send()
            for c in range(PIECES):
                pass_copy(kind, c, k).wait_send()

    over_peers(sent)


def store(*refs):
    count = len(refs) // 2
    held, out, sem = refs[:count], refs[count:-1], refs[-1]
    copies = [pltpu.make_async_copy(a, b, sem.at[i]) for i, (a, b) in enumerate(zip(held, out))]
    for copy in copies:
        copy.start()
    for copy in copies:
        copy.wait()


def shards(group_width, cycle, images, texts, scale, shift):
    rows, width = images.shape
    flops = 4 * 2 * rows * SPAN * group_width * rows * width
    shapes = (
        jax.ShapeDtypeStruct((rows, width), jnp.float32),
        jax.ShapeDtypeStruct((rows, width), jnp.float32),
        jax.ShapeDtypeStruct((1, rows), jnp.float32),
    )
    results = pl.pallas_call(
        functools.partial(kernel, group_width, cycle),
        out_shape=shapes,
        in_specs=[pl.BlockSpec(memory_space=pltpu.HBM)] * 2
        + [pl.BlockSpec(memory_space=pltpu.SMEM)] * 2,
        out_specs=[pl.BlockSpec(memory_space=pltpu.VMEM)] * 3,
        scratch_shapes=[
            pltpu.VMEM((2, group_width * rows, width), images.dtype),
            pltpu.VMEM((2, PIECES, group_width * rows // PIECES, width), images.dtype),
            pltpu.SemaphoreType.DMA((2,)),
            pltpu.SemaphoreType.DMA((2, group_width)),
            pltpu.SemaphoreType.DMA((2, group_width)),
            pltpu.SemaphoreType.DMA((2, PIECES)),
            pltpu.SemaphoreType.DMA((2, PIECES)),
            pltpu.SemaphoreType.DMA((2, PIECES, group_width)),
            pltpu.SemaphoreType.DMA((2, PIECES, group_width)),
        ],
        compiler_params=pltpu.CompilerParams(
            collective_id=0, has_side_effects=True, vmem_limit_bytes=32 << 20
        ),
        cost_estimate=pl.CostEstimate(
            flops=flops, bytes_accessed=16 * rows * width, transcendentals=0
        ),
    )(
        pltpu.with_memory_space_constraint(images, pltpu.HBM),
        pltpu.with_memory_space_constraint(texts, pltpu.HBM),
        scale,
        shift,
    )
    grad_images, grad_texts, row_loss = pl.pallas_call(
        store,
        out_shape=shapes,
        in_specs=[pl.BlockSpec(memory_space=pltpu.VMEM)] * 3,
        out_specs=[pl.BlockSpec(memory_space=pltpu.HBM)] * 3,
        scratch_shapes=[pltpu.SemaphoreType.DMA((3,))],
        compiler_params=pltpu.CompilerParams(vmem_limit_bytes=8 << 20),
        cost_estimate=pl.CostEstimate(
            flops=0, bytes_accessed=16 * rows * width, transcendentals=0
        ),
    )(*results)
    return grad_images, grad_texts, row_loss.reshape(rows)


def solution(mesh):
    placed = (P(("group", "blk"), None), P(("group", "blk"), None), P(), P())
    return jax.shard_map(
        functools.partial(shards, mesh.shape["group"], mesh.shape["blk"]),
        mesh=mesh,
        in_specs=placed,
        out_specs=(P(("group", "blk"), None), P(("group", "blk"), None), P(("group", "blk"))),
        check_vma=False,
    )
```

```python
import functools

import jax
import jax.numpy as jnp
from jax import lax
from jax.experimental import pallas as pl
from jax.experimental.pallas import tpu as pltpu
from jax.sharding import PartitionSpec as P

SPAN = 2
PIECES = 4
WINDOW = 2
TEXT, IMAGE = 0, 1


def kernel(
    group_width, cycle, images, texts, scale, shift, grad_images, grad_texts, row_loss,
    near, far, load_sem, near_send, near_recv, far_send, far_recv, pass_send, pass_recv,
):
    group, place = lax.axis_index("group"), lax.axis_index("blk")
    after, before = lax.rem(place + 1, cycle), lax.rem(place + cycle - 1, cycle)
    rows = images.shape[0]
    piece = rows // PIECES
    sources = (texts, images)
    onward = (after, before)

    def peer(k):
        return lax.rem(group + k, group_width)

    def over_peers(body):
        if group_width <= 2:
            for k in range(1, group_width):
                body(k)
        else:
            pl.loop(1, group_width)(body)

    def own(kind):
        return near.at[kind, pl.ds(pl.multiple_of(group * rows, rows), rows)]

    def own_piece(kind, c):
        return far.at[kind, c, pl.ds(pl.multiple_of(group * piece, piece), piece)]

    def loads(kind):
        return pltpu.make_async_copy(sources[kind], own(kind), load_sem.at[kind])

    def near_copy(kind, k):
        return pltpu.make_async_remote_copy(
            src_ref=sources[kind], dst_ref=own(kind),
            send_sem=near_send.at[kind, k], recv_sem=near_recv.at[kind, k],
            device_id=(peer(k), place), device_id_type=pl.DeviceIdType.MESH,
        )

    def far_copy(kind, c):
        return pltpu.make_async_remote_copy(
            src_ref=sources[kind].at[pl.ds(c * piece, piece)], dst_ref=own_piece(kind, c),
            send_sem=far_send.at[kind, c], recv_sem=far_recv.at[kind, c],
            device_id=(group, onward[kind]), device_id_type=pl.DeviceIdType.MESH,
        )

    def pass_copy(kind, c, k):
        return pltpu.make_async_remote_copy(
            src_ref=own_piece(kind, c), dst_ref=own_piece(kind, c),
            send_sem=pass_send.at[kind, c, k], recv_sem=pass_recv.at[kind, c, k],
            device_id=(peer(k), place), device_id_type=pl.DeviceIdType.MESH,
        )

    for kind in (TEXT, IMAGE):
        loads(kind).start()
    barrier = pltpu.get_barrier_semaphore()
    for neighbour in (after, before):
        pl.semaphore_signal(
            barrier, inc=1, device_id=(group, neighbour), device_id_type=pl.DeviceIdType.MESH
        )

    def greet(k):
        pl.semaphore_signal(
            barrier, inc=1, device_id=(peer(k), place), device_id_type=pl.DeviceIdType.MESH
        )

    over_peers(greet)
    pl.semaphore_wait(barrier, group_width + 1)

    for c in range(WINDOW):
        for kind in (TEXT, IMAGE):
            far_copy(kind, c).start()
    for kind in (TEXT, IMAGE):
        over_peers(lambda k: near_copy(kind, k).start())

    factor, offset = scale[0], shift[0]
    outputs = (grad_images, grad_texts)

    def meet(kind, block, first=False):
        z = lax.dot_general(
            block, own(1 - kind)[...], (((1,), (1,)), ((), ())), preferred_element_type=jnp.float32
        )
        z = factor * z + offset
        if first:
            same = lax.broadcasted_iota(jnp.int32, z.shape, 0) == (
                lax.broadcasted_iota(jnp.int32, z.shape, 1) + group * rows
            )
            z = jnp.where(same, -z, z)
        small = jnp.exp(-jnp.abs(z))
        slopes = factor * (jnp.where(z >= 0, 1.0, small) / (1.0 + small))
        if first:
            slopes = jnp.where(same, -slopes, slopes)
        if kind == TEXT:
            loss = jnp.sum(jnp.maximum(z, 0.0) + jnp.log1p(small), axis=0, keepdims=True)
            row_loss[...] = loss if first else row_loss[...] + loss
        grad = lax.dot_general(
            slopes.astype(jnp.bfloat16), block, (((0,), (0,)), ((), ())),
            preferred_element_type=jnp.float32,
        )
        out = outputs[kind]
        out[...] = grad if first else out[...] + grad

    for kind in (TEXT, IMAGE):
        loads(kind).wait()
        over_peers(lambda k: near_copy(kind, k).wait_recv())
    for kind in (TEXT, IMAGE):
        meet(kind, near[kind], first=True)

    def meet_far(c):
        for kind in (TEXT, IMAGE):
            over_peers(lambda k: pass_copy(kind, c, k).wait_recv())
        for kind in (TEXT, IMAGE):
            meet(kind, far[kind, c])

    for c in range(PIECES):
        for kind in (TEXT, IMAGE):
            far_copy(kind, c).wait_recv()
            over_peers(lambda k: pass_copy(kind, c, k).start())
        if c + WINDOW < PIECES:
            for kind in (TEXT, IMAGE):
                far_copy(kind, c).wait_send()
                far_copy(kind, c + WINDOW).start()
        if c > 0:
            meet_far(c - 1)
    meet_far(PIECES - 1)
    row_loss[...] = row_loss[...] / (SPAN * group_width * rows)

    for kind in (TEXT, IMAGE):
        for c in range(PIECES - WINDOW, PIECES):
            far_copy(kind, c).wait_send()

    def sent(k):
        for kind in (TEXT, IMAGE):
            near_copy(kind, k).wait_send()
            for c in range(PIECES):
                pass_copy(kind, c, k).wait_send()

    over_peers(sent)


def store(*refs):
    count = len(refs) // 2
    held, out, sem = refs[:count], refs[count:-1], refs[-1]
    copies = [pltpu.make_async_copy(a, b, sem.at[i]) for i, (a, b) in enumerate(zip(held, out))]
    for copy in copies:
        copy.start()
    for copy in copies:
        copy.wait()


def shards(group_width, cycle, images, texts, scale, shift):
    rows, width = images.shape
    flops = 4 * 2 * rows * SPAN * group_width * rows * width
    shapes = (
        jax.ShapeDtypeStruct((rows, width), jnp.float32),
        jax.ShapeDtypeStruct((rows, width), jnp.float32),
        jax.ShapeDtypeStruct((1, rows), jnp.float32),
    )
    results = pl.pallas_call(
        functools.partial(kernel, group_width, cycle),
        out_shape=shapes,
        in_specs=[pl.BlockSpec(memory_space=pltpu.HBM)] * 2
        + [pl.BlockSpec(memory_space=pltpu.SMEM)] * 2,
        out_specs=[pl.BlockSpec(memory_space=pltpu.VMEM)] * 3,
        scratch_shapes=[
            pltpu.VMEM((2, group_width * rows, width), images.dtype),
            pltpu.VMEM((2, PIECES, group_width * rows // PIECES, width), images.dtype),
            pltpu.SemaphoreType.DMA((2,)),
            pltpu.SemaphoreType.DMA((2, group_width)),
            pltpu.SemaphoreType.DMA((2, group_width)),
            pltpu.SemaphoreType.DMA((2, PIECES)),
            pltpu.SemaphoreType.DMA((2, PIECES)),
            pltpu.SemaphoreType.DMA((2, PIECES, group_width)),
            pltpu.SemaphoreType.DMA((2, PIECES, group_width)),
        ],
        compiler_params=pltpu.CompilerParams(
            collective_id=0, has_side_effects=True, vmem_limit_bytes=32 << 20
        ),
        cost_estimate=pl.CostEstimate(
            flops=flops, bytes_accessed=16 * rows * width, transcendentals=0
        ),
    )(
        pltpu.with_memory_space_constraint(images, pltpu.HBM),
        pltpu.with_memory_space_constraint(texts, pltpu.HBM),
        scale,
        shift,
    )
    grad_images, grad_texts, row_loss = pl.pallas_call(
        store,
        out_shape=shapes,
        in_specs=[pl.BlockSpec(memory_space=pltpu.VMEM)] * 3,
        out_specs=[pl.BlockSpec(memory_space=pltpu.HBM)] * 3,
        scratch_shapes=[pltpu.SemaphoreType.DMA((3,))],
        compiler_params=pltpu.CompilerParams(vmem_limit_bytes=8 << 20),
        cost_estimate=pl.CostEstimate(
            flops=0, bytes_accessed=16 * rows * width, transcendentals=0
        ),
    )(*results)
    return grad_images, grad_texts, row_loss.reshape(rows)


def solution(mesh):
    placed = (P(("group", "blk"), None), P(("group", "blk"), None), P(), P())
    return jax.shard_map(
        functools.partial(shards, mesh.shape["group"], mesh.shape["blk"]),
        mesh=mesh,
        in_specs=placed,
        out_specs=(P(("group", "blk"), None), P(("group", "blk"), None), P(("group", "blk"))),
        check_vma=False,
    )
```

```python
import functools

import jax
import jax.numpy as jnp
from jax import lax
from jax.experimental import pallas as pl
from jax.experimental.pallas import tpu as pltpu
from jax.sharding import PartitionSpec as P

SPAN = 2
TEXT, IMAGE = 0, 1
EIGHTHS = ((4, 4), (2, 2, 2, 1, 1))


def kernel(
    group_width, cycle, images, texts, scale, shift, grad_images, grad_texts, row_loss,
    near, far, load_sem, near_send, near_recv, far_send, far_recv, pass_send, pass_recv,
):
    group, place = lax.axis_index("group"), lax.axis_index("blk")
    after, before = lax.rem(place + 1, cycle), lax.rem(place + cycle - 1, cycle)
    rows = images.shape[0]
    travel = []
    for kind in (TEXT, IMAGE):
        start = 0
        for number, eighths in enumerate(EIGHTHS[kind]):
            travel.append((kind, number, start, eighths * rows // 8))
            start += eighths * rows // 8
    sources = (texts, images)
    onward = (after, before)

    def peer(k):
        return lax.rem(group + k, group_width)

    def over_peers(body):
        if group_width <= 2:
            for k in range(1, group_width):
                body(k)
        else:
            pl.loop(1, group_width)(body)

    def own(kind):
        return near.at[kind, pl.ds(pl.multiple_of(group * rows, rows), rows)]

    def whole_piece(part):
        kind, _, start, size = part
        return far.at[kind, pl.ds(group_width * start, group_width * size)]

    def own_piece(part):
        kind, _, start, size = part
        offset = pl.multiple_of(group_width * start + group * size, size)
        return far.at[kind, pl.ds(offset, size)]

    def loads(kind):
        return pltpu.make_async_copy(sources[kind], own(kind), load_sem.at[kind])

    def near_copy(kind, k):
        return pltpu.make_async_remote_copy(
            src_ref=sources[kind], dst_ref=own(kind),
            send_sem=near_send.at[kind, k], recv_sem=near_recv.at[kind, k],
            device_id=(peer(k), place), device_id_type=pl.DeviceIdType.MESH,
        )

    def far_copy(part):
        kind, c, start, size = part
        return pltpu.make_async_remote_copy(
            src_ref=sources[kind].at[pl.ds(start, size)], dst_ref=own_piece(part),
            send_sem=far_send.at[kind, c], recv_sem=far_recv.at[kind, c],
            device_id=(group, onward[kind]), device_id_type=pl.DeviceIdType.MESH,
        )

    def pass_copy(part, k):
        kind, c, _, _ = part
        return pltpu.make_async_remote_copy(
            src_ref=own_piece(part), dst_ref=own_piece(part),
            send_sem=pass_send.at[kind, c, k], recv_sem=pass_recv.at[kind, c, k],
            device_id=(peer(k), place), device_id_type=pl.DeviceIdType.MESH,
        )

    for kind in (TEXT, IMAGE):
        loads(kind).start()
    barrier = pltpu.get_barrier_semaphore()
    for neighbour in (after, before):
        pl.semaphore_signal(
            barrier, inc=1, device_id=(group, neighbour), device_id_type=pl.DeviceIdType.MESH
        )

    def greet(k):
        pl.semaphore_signal(
            barrier, inc=1, device_id=(peer(k), place), device_id_type=pl.DeviceIdType.MESH
        )

    over_peers(greet)
    pl.semaphore_wait(barrier, group_width + 1)

    far_copy(travel[0]).start()
    for kind in (TEXT, IMAGE):
        over_peers(lambda k: near_copy(kind, k).start())
    for part in travel[1:]:
        far_copy(part).start()

    factor, offset = scale[0], shift[0]
    outputs = (grad_images, grad_texts)

    def meet(kind, block, first=False):
        z = lax.dot_general(
            block, own(1 - kind)[...], (((1,), (1,)), ((), ())), preferred_element_type=jnp.float32
        )
        z = factor * z + offset
        if first:
            same = lax.broadcasted_iota(jnp.int32, z.shape, 0) == (
                lax.broadcasted_iota(jnp.int32, z.shape, 1) + group * rows
            )
            z = jnp.where(same, -z, z)
        small = jnp.exp(-jnp.abs(z))
        slopes = factor * (jnp.where(z >= 0, 1.0, small) / (1.0 + small))
        if first:
            slopes = jnp.where(same, -slopes, slopes)
        if kind == TEXT:
            loss = jnp.sum(jnp.maximum(z, 0.0) + jnp.log1p(small), axis=0, keepdims=True)
            row_loss[...] = loss if first else row_loss[...] + loss
        grad = lax.dot_general(
            slopes.astype(jnp.bfloat16), block, (((0,), (0,)), ((), ())),
            preferred_element_type=jnp.float32,
        )
        out = outputs[kind]
        out[...] = grad if first else out[...] + grad

    for kind in (TEXT, IMAGE):
        loads(kind).wait()
        over_peers(lambda k: near_copy(kind, k).wait_recv())
    for kind in (TEXT, IMAGE):
        meet(kind, near[kind], first=True)

    def meet_far(part):
        over_peers(lambda k: pass_copy(part, k).wait_recv())
        meet(part[0], whole_piece(part)[...])

    earlier = None
    for part in travel:
        far_copy(part).wait_recv()
        over_peers(lambda k: pass_copy(part, k).start())
        if earlier is not None:
            meet_far(earlier)
        earlier = part
    meet_far(earlier)
    row_loss[...] = row_loss[...] / (SPAN * group_width * rows)

    for part in travel:
        far_copy(part).wait_send()

    def sent(k):
        for kind in (TEXT, IMAGE):
            near_copy(kind, k).wait_send()
        for part in travel:
            pass_copy(part, k).wait_send()

    over_peers(sent)


def store(*refs):
    count = len(refs) // 2
    held, out, sem = refs[:count], refs[count:-1], refs[-1]
    copies = [pltpu.make_async_copy(a, b, sem.at[i]) for i, (a, b) in enumerate(zip(held, out))]
    for copy in copies:
        copy.start()
    for copy in copies:
        copy.wait()


def shards(group_width, cycle, images, texts, scale, shift):
    rows, width = images.shape
    flops = 4 * 2 * rows * SPAN * group_width * rows * width
    most = max(len(pieces) for pieces in EIGHTHS)
    shapes = (
        jax.ShapeDtypeStruct((rows, width), jnp.float32),
        jax.ShapeDtypeStruct((rows, width), jnp.float32),
        jax.ShapeDtypeStruct((1, rows), jnp.float32),
    )
    results = pl.pallas_call(
        functools.partial(kernel, group_width, cycle),
        out_shape=shapes,
        in_specs=[pl.BlockSpec(memory_space=pltpu.HBM)] * 2
        + [pl.BlockSpec(memory_space=pltpu.SMEM)] * 2,
        out_specs=[pl.BlockSpec(memory_space=pltpu.VMEM)] * 3,
        scratch_shapes=[
            pltpu.VMEM((2, group_width * rows, width), images.dtype),
            pltpu.VMEM((2, group_width * rows, width), images.dtype),
            pltpu.SemaphoreType.DMA((2,)),
            pltpu.SemaphoreType.DMA((2, group_width)),
            pltpu.SemaphoreType.DMA((2, group_width)),
            pltpu.SemaphoreType.DMA((2, most)),
            pltpu.SemaphoreType.DMA((2, most)),
            pltpu.SemaphoreType.DMA((2, most, group_width)),
            pltpu.SemaphoreType.DMA((2, most, group_width)),
        ],
        compiler_params=pltpu.CompilerParams(
            collective_id=0, has_side_effects=True, vmem_limit_bytes=32 << 20
        ),
        cost_estimate=pl.CostEstimate(
            flops=flops, bytes_accessed=16 * rows * width, transcendentals=0
        ),
    )(
        pltpu.with_memory_space_constraint(images, pltpu.HBM),
        pltpu.with_memory_space_constraint(texts, pltpu.HBM),
        scale,
        shift,
    )
    grad_images, grad_texts, row_loss = pl.pallas_call(
        store,
        out_shape=shapes,
        in_specs=[pl.BlockSpec(memory_space=pltpu.VMEM)] * 3,
        out_specs=[pl.BlockSpec(memory_space=pltpu.HBM)] * 3,
        scratch_shapes=[pltpu.SemaphoreType.DMA((3,))],
        compiler_params=pltpu.CompilerParams(vmem_limit_bytes=8 << 20),
        cost_estimate=pl.CostEstimate(
            flops=0, bytes_accessed=16 * rows * width, transcendentals=0
        ),
    )(*results)
    return grad_images, grad_texts, row_loss.reshape(rows)


def solution(mesh):
    placed = (P(("group", "blk"), None), P(("group", "blk"), None), P(), P())
    return jax.shard_map(
        functools.partial(shards, mesh.shape["group"], mesh.shape["blk"]),
        mesh=mesh,
        in_specs=placed,
        out_specs=(P(("group", "blk"), None), P(("group", "blk"), None), P(("group", "blk"))),
        check_vma=False,
    )
```

```python
import functools

import jax
import jax.numpy as jnp
from jax import lax
from jax.experimental import pallas as pl
from jax.experimental.pallas import tpu as pltpu
from jax.sharding import PartitionSpec as P

SPAN = 2
TEXT, IMAGE = 0, 1
VIA, DIRECT = (2, 2, 2, 2), (2, 2, 2, 1, 1)
TURNS = "r0 T0 r1 I0 r2 v0 r3 v1 V0 v2 V1 d0 v3 V2 D0 d1 V3 d2 D1 d3 D2 d4 D3 D4"


def pieces(eighths, rows):
    parts, start = [], 0
    for share in eighths:
        parts.append((start, share * rows // 8))
        start += share * rows // 8
    return parts


def kernel(
    group_width, cycle, images, texts, scale, shift, grads, row_loss,
    near, relay, via, direct, losses, load_sem, near_send, near_recv, out_send, out_recv,
    on_send, on_recv, via_send, via_recv, pass_send, pass_recv,
):
    group, place = lax.axis_index("group"), lax.axis_index("blk")
    odd = lax.rem(place, 2)
    partner = place + 1 - 2 * odd
    onward = lax.rem(place + cycle + 2 - 4 * odd, cycle)
    behind = lax.rem(place + cycle - 2 + 4 * odd, cycle)
    via_kind, direct_kind = odd, 1 - odd
    rows = images.shape[0]
    via_parts, direct_parts = pieces(VIA, rows), pieces(DIRECT, rows)

    def peer(k):
        return lax.rem(group + k, group_width)

    def over_peers(body):
        if group_width <= 2:
            for k in range(1, group_width):
                body(k)
        else:
            pl.loop(1, group_width)(body)

    def remote(src, dst, send, recv, device):
        return pltpu.make_async_remote_copy(
            src_ref=src, dst_ref=dst, send_sem=send, recv_sem=recv,
            device_id=device, device_id_type=pl.DeviceIdType.MESH,
        )

    def own(kind, start=0, size=rows):
        return near.at[kind, pl.ds(pl.multiple_of(group * rows + start, size), size)]

    def mine(block, part):
        start, size = part
        return block.at[pl.ds(pl.multiple_of(group_width * start + group * size, size), size)]

    def load(kind):
        return pltpu.make_async_copy((texts, images)[kind], own(kind), load_sem.at[kind])

    def near_copy(kind, k):
        return remote(
            own(kind), own(kind), near_send.at[kind, k], near_recv.at[kind, k], (peer(k), place)
        )

    def first_copy(c):
        start, size = via_parts[c]
        return remote(
            own(1 - odd, start, size), relay.at[pl.ds(start, size)],
            out_send.at[c], out_recv.at[c], (group, partner),
        )

    def onward_copy(c):
        start, size = via_parts[c]
        return remote(
            relay.at[pl.ds(start, size)], mine(via, via_parts[c]),
            on_send.at[c], on_recv.at[c], (group, onward),
        )

    def direct_copy(c):
        start, size = direct_parts[c]
        return remote(
            own(odd, start, size), mine(direct, direct_parts[c]),
            via_send.at[c], via_recv.at[c], (group, partner),
        )

    def pass_copy(which, c, k):
        block = mine(direct, direct_parts[c]) if which else mine(via, via_parts[c])
        return remote(
            block, block, pass_send.at[which, c, k], pass_recv.at[which, c, k], (peer(k), place)
        )

    for kind in (TEXT, IMAGE):
        load(kind).start()
    barrier = pltpu.get_barrier_semaphore()

    def greet(device):
        pl.semaphore_signal(
            barrier, inc=1, device_id=device, device_id_type=pl.DeviceIdType.MESH
        )

    greet((group, behind))
    greet((group, partner))
    over_peers(lambda k: greet((peer(k), place)))
    for kind in (TEXT, IMAGE):
        load(kind).wait()
    pl.semaphore_wait(barrier, group_width + 1)

    for c in range(len(VIA)):
        first_copy(c).start()
    for kind in (TEXT, IMAGE):
        over_peers(lambda k: near_copy(kind, k).start())
    for c in range(len(DIRECT)):
        direct_copy(c).start()

    factor, offset = scale[0], shift[0]

    def meet(kind, block, first=False):
        z = lax.dot_general(
            block, own(1 - kind)[...], (((1,), (1,)), ((), ())),
            preferred_element_type=jnp.float32,
        )
        z = factor * z + offset
        if first:
            same = lax.broadcasted_iota(jnp.int32, z.shape, 0) == (
                lax.broadcasted_iota(jnp.int32, z.shape, 1) + group * rows
            )
            z = jnp.where(same, -z, z)
        small = jnp.exp(-jnp.abs(z))
        slopes = factor * (jnp.where(z >= 0, 1.0, small) / (1.0 + small))
        if first:
            slopes = jnp.where(same, -slopes, slopes)
        loss = jnp.sum(jnp.maximum(z, 0.0) + jnp.log1p(small), axis=0, keepdims=True)
        grad = lax.dot_general(
            slopes.astype(jnp.bfloat16), block, (((0,), (0,)), ((), ())),
            preferred_element_type=jnp.float32,
        )
        losses[kind] = loss if first else losses[kind] + loss
        grads[kind] = grad if first else grads[kind] + grad

    for turn in TURNS.split():
        what, c = turn[0], int(turn[1:])
        if what == "r":
            first_copy(c).wait_recv()
            onward_copy(c).start()
        elif what in "vd":
            (direct_copy if what == "d" else onward_copy)(c).wait_recv()
            over_peers(lambda k: pass_copy(int(what == "d"), c, k).start())
        elif what in "VD":
            over_peers(lambda k: pass_copy(int(what == "D"), c, k).wait_recv())
            block, kind = (direct, direct_kind) if what == "D" else (via, via_kind)
            start, size = (direct_parts if what == "D" else via_parts)[c]
            meet(kind, block[pl.ds(group_width * start, group_width * size)])
        else:
            kind = TEXT if what == "T" else IMAGE
            if kind == TEXT:
                for each in (TEXT, IMAGE):
                    over_peers(lambda k: near_copy(each, k).wait_recv())
            meet(kind, near[kind], first=True)
    row_loss[...] = losses[TEXT] / (SPAN * group_width * rows)

    for c in range(len(VIA)):
        first_copy(c).wait_send()
        onward_copy(c).wait_send()
    for c in range(len(DIRECT)):
        direct_copy(c).wait_send()

    def sent(k):
        for kind in (TEXT, IMAGE):
            near_copy(kind, k).wait_send()
        for which, count in ((0, len(VIA)), (1, len(DIRECT))):
            for c in range(count):
                pass_copy(which, c, k).wait_send()

    over_peers(sent)


def store(grads, held_loss, grad_images, grad_texts, row_loss, sem):
    moves = ((grads.at[0], grad_images), (grads.at[1], grad_texts), (held_loss, row_loss))
    copies = [pltpu.make_async_copy(a, b, sem.at[i]) for i, (a, b) in enumerate(moves)]
    for copy in copies:
        copy.start()
    for copy in copies:
        copy.wait()


def shards(group_width, cycle, images, texts, scale, shift):
    rows, width = images.shape
    flops = 4 * 2 * rows * SPAN * group_width * rows * width
    most = max(len(VIA), len(DIRECT))
    results = pl.pallas_call(
        functools.partial(kernel, group_width, cycle),
        out_shape=(
            jax.ShapeDtypeStruct((2, rows, width), jnp.float32),
            jax.ShapeDtypeStruct((1, rows), jnp.float32),
        ),
        in_specs=[pl.BlockSpec(memory_space=pltpu.HBM)] * 2
        + [pl.BlockSpec(memory_space=pltpu.SMEM)] * 2,
        out_specs=[pl.BlockSpec(memory_space=pltpu.VMEM)] * 2,
        scratch_shapes=[
            pltpu.VMEM((2, group_width * rows, width), images.dtype),
            pltpu.VMEM((rows, width), images.dtype),
            pltpu.VMEM((group_width * rows, width), images.dtype),
            pltpu.VMEM((group_width * rows, width), images.dtype),
            pltpu.VMEM((2, 1, rows), jnp.float32),
            pltpu.SemaphoreType.DMA((2,)),
            pltpu.SemaphoreType.DMA((2, group_width)),
            pltpu.SemaphoreType.DMA((2, group_width)),
        ]
        + [pltpu.SemaphoreType.DMA((most,))] * 6
        + [pltpu.SemaphoreType.DMA((2, most, group_width))] * 2,
        compiler_params=pltpu.CompilerParams(
            collective_id=0, has_side_effects=True, vmem_limit_bytes=32 << 20
        ),
        cost_estimate=pl.CostEstimate(
            flops=flops, bytes_accessed=16 * rows * width, transcendentals=0
        ),
    )(
        pltpu.with_memory_space_constraint(images, pltpu.HBM),
        pltpu.with_memory_space_constraint(texts, pltpu.HBM),
        scale,
        shift,
    )
    grad_images, grad_texts, row_loss = pl.pallas_call(
        store,
        out_shape=(
            jax.ShapeDtypeStruct((rows, width), jnp.float32),
            jax.ShapeDtypeStruct((rows, width), jnp.float32),
            jax.ShapeDtypeStruct((1, rows), jnp.float32),
        ),
        in_specs=[pl.BlockSpec(memory_space=pltpu.VMEM)] * 2,
        out_specs=[pl.BlockSpec(memory_space=pltpu.HBM)] * 3,
        scratch_shapes=[pltpu.SemaphoreType.DMA((3,))],
        compiler_params=pltpu.CompilerParams(vmem_limit_bytes=8 << 20),
        cost_estimate=pl.CostEstimate(
            flops=0, bytes_accessed=16 * rows * width, transcendentals=0
        ),
    )(*results)
    return grad_images, grad_texts, row_loss.reshape(rows)


def solution(mesh):
    placed = (P(("group", "blk"), None), P(("group", "blk"), None), P(), P())
    return jax.shard_map(
        functools.partial(shards, mesh.shape["group"], mesh.shape["blk"]),
        mesh=mesh,
        in_specs=placed,
        out_specs=(P(("group", "blk"), None), P(("group", "blk"), None), P(("group", "blk"))),
        check_vma=False,
    )
```

```python
import functools

import jax
import jax.numpy as jnp
from jax import lax
from jax.experimental import pallas as pl
from jax.experimental.pallas import tpu as pltpu
from jax.sharding import PartitionSpec as P

SPAN = 2
TEXT, IMAGE = 0, 1
EIGHTHS = (2, 2, 2, 1, 1)


def kernel(
    group_width, cycle, images, texts, scale, shift, grad_images, grad_texts, row_loss,
    near, far, load_sem, near_send, near_recv, far_send, far_recv, pass_send, pass_recv,
):
    group, place = lax.axis_index("group"), lax.axis_index("blk")
    after, before = lax.rem(place + 1, cycle), lax.rem(place + cycle - 1, cycle)
    rows = images.shape[0]
    travel = []
    start = 0
    for number, eighths in enumerate(EIGHTHS):
        size = eighths * rows // 8
        travel += [(kind, number, start, size) for kind in (TEXT, IMAGE)]
        start += size
    sources = (texts, images)
    onward = (after, before)

    def peer(k):
        return lax.rem(group + k, group_width)

    def over_peers(body):
        if group_width <= 2:
            for k in range(1, group_width):
                body(k)
        else:
            pl.loop(1, group_width)(body)

    def own(kind):
        return near.at[kind, pl.ds(pl.multiple_of(group * rows, rows), rows)]

    def whole_piece(part):
        kind, _, start, size = part
        return far.at[kind, pl.ds(group_width * start, group_width * size)]

    def own_piece(part):
        kind, _, start, size = part
        offset = pl.multiple_of(group_width * start + group * size, size)
        return far.at[kind, pl.ds(offset, size)]

    def loads(kind):
        return pltpu.make_async_copy(sources[kind], own(kind), load_sem.at[kind])

    def near_copy(kind, k):
        return pltpu.make_async_remote_copy(
            src_ref=sources[kind], dst_ref=own(kind),
            send_sem=near_send.at[kind, k], recv_sem=near_recv.at[kind, k],
            device_id=(peer(k), place), device_id_type=pl.DeviceIdType.MESH,
        )

    def far_copy(part):
        kind, c, start, size = part
        return pltpu.make_async_remote_copy(
            src_ref=sources[kind].at[pl.ds(start, size)], dst_ref=own_piece(part),
            send_sem=far_send.at[kind, c], recv_sem=far_recv.at[kind, c],
            device_id=(group, onward[kind]), device_id_type=pl.DeviceIdType.MESH,
        )

    def pass_copy(part, k):
        kind, c, _, _ = part
        return pltpu.make_async_remote_copy(
            src_ref=own_piece(part), dst_ref=own_piece(part),
            send_sem=pass_send.at[kind, c, k], recv_sem=pass_recv.at[kind, c, k],
            device_id=(peer(k), place), device_id_type=pl.DeviceIdType.MESH,
        )

    for kind in (TEXT, IMAGE):
        loads(kind).start()
    barrier = pltpu.get_barrier_semaphore()
    for neighbour in (after, before):
        pl.semaphore_signal(
            barrier, inc=1, device_id=(group, neighbour), device_id_type=pl.DeviceIdType.MESH
        )

    def greet(k):
        pl.semaphore_signal(
            barrier, inc=1, device_id=(peer(k), place), device_id_type=pl.DeviceIdType.MESH
        )

    over_peers(greet)
    pl.semaphore_wait(barrier, group_width + 1)

    for kind in (TEXT, IMAGE):
        over_peers(lambda k: near_copy(kind, k).start())
    for part in travel:
        far_copy(part).start()

    factor, offset = scale[0], shift[0]
    outputs = (grad_images, grad_texts)

    def meet(kind, block, first=False):
        z = lax.dot_general(
            block, own(1 - kind)[...], (((1,), (1,)), ((), ())), preferred_element_type=jnp.float32
        )
        z = factor * z + offset
        if first:
            same = lax.broadcasted_iota(jnp.int32, z.shape, 0) == (
                lax.broadcasted_iota(jnp.int32, z.shape, 1) + group * rows
            )
            z = jnp.where(same, -z, z)
        small = jnp.exp(-jnp.abs(z))
        slopes = factor * (jnp.where(z >= 0, 1.0, small) / (1.0 + small))
        if first:
            slopes = jnp.where(same, -slopes, slopes)
        if kind == TEXT:
            loss = jnp.sum(jnp.maximum(z, 0.0) + jnp.log1p(small), axis=0, keepdims=True)
            row_loss[...] = loss if first else row_loss[...] + loss
        grad = lax.dot_general(
            slopes.astype(jnp.bfloat16), block, (((0,), (0,)), ((), ())),
            preferred_element_type=jnp.float32,
        )
        out = outputs[kind]
        out[...] = grad if first else out[...] + grad

    for kind in (TEXT, IMAGE):
        loads(kind).wait()
        over_peers(lambda k: near_copy(kind, k).wait_recv())
    for kind in (TEXT, IMAGE):
        meet(kind, near[kind], first=True)

    def meet_far(*parts):
        for part in parts:
            over_peers(lambda k: pass_copy(part, k).wait_recv())
        for part in parts:
            meet(part[0], whole_piece(part)[...])

    def pass_on(part):
        far_copy(part).wait_recv()
        over_peers(lambda k: pass_copy(part, k).start())

    for i in range(0, len(travel), 2):
        pass_on(travel[i])
        pass_on(travel[i + 1])
        if i > 0:
            meet_far(travel[i - 2], travel[i - 1])
    meet_far(travel[-2], travel[-1])
    row_loss[...] = row_loss[...] / (SPAN * group_width * rows)

    for part in travel:
        far_copy(part).wait_send()

    def sent(k):
        for kind in (TEXT, IMAGE):
            near_copy(kind, k).wait_send()
        for part in travel:
            pass_copy(part, k).wait_send()

    over_peers(sent)


def store(*refs):
    count = len(refs) // 2
    held, out, sem = refs[:count], refs[count:-1], refs[-1]
    copies = [pltpu.make_async_copy(a, b, sem.at[i]) for i, (a, b) in enumerate(zip(held, out))]
    for copy in copies:
        copy.start()
    for copy in copies:
        copy.wait()


def shards(group_width, cycle, images, texts, scale, shift):
    rows, width = images.shape
    flops = 4 * 2 * rows * SPAN * group_width * rows * width
    shapes = (
        jax.ShapeDtypeStruct((rows, width), jnp.float32),
        jax.ShapeDtypeStruct((rows, width), jnp.float32),
        jax.ShapeDtypeStruct((1, rows), jnp.float32),
    )
    results = pl.pallas_call(
        functools.partial(kernel, group_width, cycle),
        out_shape=shapes,
        in_specs=[pl.BlockSpec(memory_space=pltpu.HBM)] * 2
        + [pl.BlockSpec(memory_space=pltpu.SMEM)] * 2,
        out_specs=[pl.BlockSpec(memory_space=pltpu.VMEM)] * 3,
        scratch_shapes=[
            pltpu.VMEM((2, group_width * rows, width), images.dtype),
            pltpu.VMEM((2, group_width * rows, width), images.dtype),
            pltpu.SemaphoreType.DMA((2,)),
            pltpu.SemaphoreType.DMA((2, group_width)),
            pltpu.SemaphoreType.DMA((2, group_width)),
            pltpu.SemaphoreType.DMA((2, len(EIGHTHS))),
            pltpu.SemaphoreType.DMA((2, len(EIGHTHS))),
            pltpu.SemaphoreType.DMA((2, len(EIGHTHS), group_width)),
            pltpu.SemaphoreType.DMA((2, len(EIGHTHS), group_width)),
        ],
        compiler_params=pltpu.CompilerParams(
            collective_id=0, has_side_effects=True, vmem_limit_bytes=32 << 20
        ),
        cost_estimate=pl.CostEstimate(
            flops=flops, bytes_accessed=16 * rows * width, transcendentals=0
        ),
    )(
        pltpu.with_memory_space_constraint(images, pltpu.HBM),
        pltpu.with_memory_space_constraint(texts, pltpu.HBM),
        scale,
        shift,
    )
    grad_images, grad_texts, row_loss = pl.pallas_call(
        store,
        out_shape=shapes,
        in_specs=[pl.BlockSpec(memory_space=pltpu.VMEM)] * 3,
        out_specs=[pl.BlockSpec(memory_space=pltpu.HBM)] * 3,
        scratch_shapes=[pltpu.SemaphoreType.DMA((3,))],
        compiler_params=pltpu.CompilerParams(vmem_limit_bytes=8 << 20),
        cost_estimate=pl.CostEstimate(
            flops=0, bytes_accessed=16 * rows * width, transcendentals=0
        ),
    )(*results)
    return grad_images, grad_texts, row_loss.reshape(rows)


def solution(mesh):
    placed = (P(("group", "blk"), None), P(("group", "blk"), None), P(), P())
    return jax.shard_map(
        functools.partial(shards, mesh.shape["group"], mesh.shape["blk"]),
        mesh=mesh,
        in_specs=placed,
        out_specs=(P(("group", "blk"), None), P(("group", "blk"), None), P(("group", "blk"))),
        check_vma=False,
    )
```

```python
import functools

import jax
import jax.numpy as jnp
from jax import lax
from jax.experimental import pallas as pl
from jax.experimental.pallas import tpu as pltpu
from jax.sharding import PartitionSpec as P

SPAN = 2
TEXT, IMAGE = 0, 1
EIGHTHS = (4, 2, 1, 1)


def kernel(
    group_width, cycle, images, texts, scale, shift, grad_images, grad_texts, row_loss,
    near, far, sums, going, coming, losses, losses_in, load_sem, near_send, near_recv,
    far_send, far_recv, sum_send, sum_recv, loss_send, loss_recv,
):
    group, place = lax.axis_index("group"), lax.axis_index("blk")
    after, before = lax.rem(place + 1, cycle), lax.rem(place + cycle - 1, cycle)
    rows = images.shape[0]
    travel = []
    start = 0
    for number, eighths in enumerate(EIGHTHS):
        size = eighths * rows // 8
        travel += [(kind, number, start, size) for kind in (TEXT, IMAGE)]
        start += size
    sources = (texts, images)
    onward = (after, before)

    def peer(k):
        return lax.rem(group + k, group_width)

    def over_peers(body):
        if group_width <= 2:
            for k in range(1, group_width):
                body(k)
        else:
            pl.loop(1, group_width)(body)

    def own(kind):
        return near.at[kind, pl.ds(pl.multiple_of(group * rows, rows), rows)]

    def loads(kind):
        return pltpu.make_async_copy(sources[kind], own(kind), load_sem.at[kind])

    def near_copy(kind, k):
        return pltpu.make_async_remote_copy(
            src_ref=sources[kind], dst_ref=own(kind),
            send_sem=near_send.at[kind, k], recv_sem=near_recv.at[kind, k],
            device_id=(peer(k), place), device_id_type=pl.DeviceIdType.MESH,
        )

    def far_copy(part):
        kind, c, start, size = part
        piece = pl.ds(start, size)
        return pltpu.make_async_remote_copy(
            src_ref=sources[kind].at[piece], dst_ref=far.at[kind, piece],
            send_sem=far_send.at[kind, c], recv_sem=far_recv.at[kind, c],
            device_id=(group, onward[kind]), device_id_type=pl.DeviceIdType.MESH,
        )

    def sum_copy(kind, k):
        return pltpu.make_async_remote_copy(
            src_ref=going.at[kind, k], dst_ref=coming.at[kind, k],
            send_sem=sum_send.at[kind, k], recv_sem=sum_recv.at[kind, k],
            device_id=(peer(k), place), device_id_type=pl.DeviceIdType.MESH,
        )

    def loss_copy(k):
        return pltpu.make_async_remote_copy(
            src_ref=losses.at[peer(k)], dst_ref=losses_in.at[k],
            send_sem=loss_send.at[k], recv_sem=loss_recv.at[k],
            device_id=(peer(k), place), device_id_type=pl.DeviceIdType.MESH,
        )

    for kind in (TEXT, IMAGE):
        loads(kind).start()
    barrier = pltpu.get_barrier_semaphore()
    for neighbour in (after, before):
        pl.semaphore_signal(
            barrier, inc=1, device_id=(group, neighbour), device_id_type=pl.DeviceIdType.MESH
        )

    def greet(k):
        pl.semaphore_signal(
            barrier, inc=1, device_id=(peer(k), place), device_id_type=pl.DeviceIdType.MESH
        )

    over_peers(greet)
    pl.semaphore_wait(barrier, group_width + 1)

    for kind in (TEXT, IMAGE):
        over_peers(lambda k: near_copy(kind, k).start())
    for part in travel:
        far_copy(part).start()

    factor, offset = scale[0], shift[0]
    outputs = (grad_images, grad_texts)

    def products(block, others, diagonal=False):
        z = lax.dot_general(
            block, others, (((1,), (1,)), ((), ())), preferred_element_type=jnp.float32
        )
        z = factor * z + offset
        if diagonal:
            same = lax.broadcasted_iota(jnp.int32, z.shape, 0) == (
                lax.broadcasted_iota(jnp.int32, z.shape, 1) + group * rows
            )
            z = jnp.where(same, -z, z)
        small = jnp.exp(-jnp.abs(z))
        slopes = factor * (jnp.where(z >= 0, 1.0, small) / (1.0 + small))
        if diagonal:
            slopes = jnp.where(same, -slopes, slopes)
        loss = jnp.maximum(z, 0.0) + jnp.log1p(small)
        grad = lax.dot_general(
            slopes.astype(jnp.bfloat16), block, (((0,), (0,)), ((), ())),
            preferred_element_type=jnp.float32,
        )
        return jnp.sum(loss, axis=0, keepdims=True), grad

    def meet_near(kind):
        loss, outputs[kind][...] = products(near[kind], own(1 - kind)[...], diagonal=True)
        if kind == TEXT:
            row_loss[...] = loss

    def meet_far(part):
        kind, c, start, size = part
        far_copy(part).wait_recv()
        loss, grad = products(far[kind, pl.ds(start, size)], near[1 - kind])
        sums[kind] = grad if c == 0 else sums[kind] + grad
        if kind == TEXT:
            for s in range(group_width):
                one = loss[:, s * rows : (s + 1) * rows]
                one = jnp.broadcast_to(one, losses.shape[1:])
                losses[s] = one if c == 0 else losses[s] + one

    def block_of(s):
        return pl.ds(pl.multiple_of(s * rows, rows), rows)

    def send_sums(kind):
        def one(k):
            going[kind, k] = sums[kind, block_of(peer(k))].astype(jnp.bfloat16)
            sum_copy(kind, k).start()
            if kind == TEXT:
                loss_copy(k).start()

        over_peers(one)
        outputs[kind][...] += sums[kind, block_of(group)]
        if kind == TEXT:
            row_loss[...] += losses[group, pl.ds(0, 1)]

    def take_sums(kind):
        def one(k):
            sum_copy(kind, k).wait_recv()
            outputs[kind][...] += coming[kind, k].astype(jnp.float32)
            if kind == TEXT:
                loss_copy(k).wait_recv()
                row_loss[...] += losses_in[k, pl.ds(0, 1)]

        over_peers(one)

    for kind in (TEXT, IMAGE):
        loads(kind).wait()
        over_peers(lambda k: near_copy(kind, k).wait_recv())
    for kind in (TEXT, IMAGE):
        meet_near(kind)
    for part in travel:
        meet_far(part)
        if part[1] == len(EIGHTHS) - 1:
            send_sums(part[0])
    for kind in (TEXT, IMAGE):
        take_sums(kind)
    row_loss[...] = row_loss[...] / (SPAN * group_width * rows)

    for part in travel:
        far_copy(part).wait_send()

    def sent(k):
        for kind in (TEXT, IMAGE):
            near_copy(kind, k).wait_send()
            sum_copy(kind, k).wait_send()
        loss_copy(k).wait_send()

    over_peers(sent)


def store(*refs):
    count = len(refs) // 2
    held, out, sem = refs[:count], refs[count:-1], refs[-1]
    copies = [pltpu.make_async_copy(a, b, sem.at[i]) for i, (a, b) in enumerate(zip(held, out))]
    for copy in copies:
        copy.start()
    for copy in copies:
        copy.wait()


def shards(group_width, cycle, images, texts, scale, shift):
    rows, width = images.shape
    flops = 4 * 2 * rows * SPAN * group_width * rows * width
    shapes = (
        jax.ShapeDtypeStruct((rows, width), jnp.float32),
        jax.ShapeDtypeStruct((rows, width), jnp.float32),
        jax.ShapeDtypeStruct((1, rows), jnp.float32),
    )
    results = pl.pallas_call(
        functools.partial(kernel, group_width, cycle),
        out_shape=shapes,
        in_specs=[pl.BlockSpec(memory_space=pltpu.HBM)] * 2
        + [pl.BlockSpec(memory_space=pltpu.SMEM)] * 2,
        out_specs=[pl.BlockSpec(memory_space=pltpu.VMEM)] * 3,
        scratch_shapes=[
            pltpu.VMEM((2, group_width * rows, width), images.dtype),
            pltpu.VMEM((2, rows, width), images.dtype),
            pltpu.VMEM((2, group_width * rows, width), jnp.float32),
            pltpu.VMEM((2, group_width, rows, width), jnp.bfloat16),
            pltpu.VMEM((2, group_width, rows, width), jnp.bfloat16),
            pltpu.VMEM((group_width, 8, rows), jnp.float32),
            pltpu.VMEM((group_width, 8, rows), jnp.float32),
            pltpu.SemaphoreType.DMA((2,)),
            pltpu.SemaphoreType.DMA((2, group_width)),
            pltpu.SemaphoreType.DMA((2, group_width)),
            pltpu.SemaphoreType.DMA((2, len(EIGHTHS))),
            pltpu.SemaphoreType.DMA((2, len(EIGHTHS))),
            pltpu.SemaphoreType.DMA((2, group_width)),
            pltpu.SemaphoreType.DMA((2, group_width)),
            pltpu.SemaphoreType.DMA((group_width,)),
            pltpu.SemaphoreType.DMA((group_width,)),
        ],
        compiler_params=pltpu.CompilerParams(
            collective_id=0, has_side_effects=True, vmem_limit_bytes=32 << 20
        ),
        cost_estimate=pl.CostEstimate(
            flops=flops, bytes_accessed=16 * rows * width, transcendentals=0
        ),
    )(
        pltpu.with_memory_space_constraint(images, pltpu.HBM),
        pltpu.with_memory_space_constraint(texts, pltpu.HBM),
        scale,
        shift,
    )
    grad_images, grad_texts, row_loss = pl.pallas_call(
        store,
        out_shape=shapes,
        in_specs=[pl.BlockSpec(memory_space=pltpu.VMEM)] * 3,
        out_specs=[pl.BlockSpec(memory_space=pltpu.HBM)] * 3,
        scratch_shapes=[pltpu.SemaphoreType.DMA((3,))],
        compiler_params=pltpu.CompilerParams(vmem_limit_bytes=8 << 20),
        cost_estimate=pl.CostEstimate(
            flops=0, bytes_accessed=16 * rows * width, transcendentals=0
        ),
    )(*results)
    return grad_images, grad_texts, row_loss.reshape(rows)


def solution(mesh):
    placed = (P(("group", "blk"), None), P(("group", "blk"), None), P(), P())
    return jax.shard_map(
        functools.partial(shards, mesh.shape["group"], mesh.shape["blk"]),
        mesh=mesh,
        in_specs=placed,
        out_specs=(P(("group", "blk"), None), P(("group", "blk"), None), P(("group", "blk"))),
        check_vma=False,
    )
```

```python
import functools

import jax
import jax.numpy as jnp
from jax import lax
from jax.experimental import pallas as pl
from jax.experimental.pallas import tpu as pltpu
from jax.sharding import PartitionSpec as P

SPAN = 2
TEXT, IMAGE = 0, 1
EIGHTHS = (4, 2, 1, 1)


def kernel(
    group_width, cycle, images, texts, scale, shift, grad_images, grad_texts, row_loss,
    near, far, load_sem, near_send, near_recv, far_send, far_recv, pass_send, pass_recv,
):
    group, place = lax.axis_index("group"), lax.axis_index("blk")
    after, before = lax.rem(place + 1, cycle), lax.rem(place + cycle - 1, cycle)
    rows = images.shape[0]
    travel = []
    start = 0
    for number, eighths in enumerate(EIGHTHS):
        size = eighths * rows // 8
        travel += [(kind, number, start, size) for kind in (TEXT, IMAGE)]
        start += size
    sources = (texts, images)
    onward = (after, before)

    def peer(k):
        return lax.rem(group + k, group_width)

    def over_peers(body):
        if group_width <= 2:
            for k in range(1, group_width):
                body(k)
        else:
            pl.loop(1, group_width)(body)

    def own(kind):
        return near.at[kind, pl.ds(pl.multiple_of(group * rows, rows), rows)]

    def whole_piece(part):
        kind, _, start, size = part
        return far.at[kind, pl.ds(group_width * start, group_width * size)]

    def own_piece(part):
        kind, _, start, size = part
        offset = pl.multiple_of(group_width * start + group * size, size)
        return far.at[kind, pl.ds(offset, size)]

    def loads(kind):
        return pltpu.make_async_copy(sources[kind], own(kind), load_sem.at[kind])

    def near_copy(kind, k):
        return pltpu.make_async_remote_copy(
            src_ref=sources[kind], dst_ref=own(kind),
            send_sem=near_send.at[kind, k], recv_sem=near_recv.at[kind, k],
            device_id=(peer(k), place), device_id_type=pl.DeviceIdType.MESH,
        )

    def far_copy(part):
        kind, c, start, size = part
        return pltpu.make_async_remote_copy(
            src_ref=sources[kind].at[pl.ds(start, size)], dst_ref=own_piece(part),
            send_sem=far_send.at[kind, c], recv_sem=far_recv.at[kind, c],
            device_id=(group, onward[kind]), device_id_type=pl.DeviceIdType.MESH,
        )

    def pass_copy(part, k):
        kind, c, _, _ = part
        return pltpu.make_async_remote_copy(
            src_ref=own_piece(part), dst_ref=own_piece(part),
            send_sem=pass_send.at[kind, c, k], recv_sem=pass_recv.at[kind, c, k],
            device_id=(peer(k), place), device_id_type=pl.DeviceIdType.MESH,
        )

    for kind in (TEXT, IMAGE):
        loads(kind).start()
    barrier = pltpu.get_barrier_semaphore()
    for neighbour in (after, before):
        pl.semaphore_signal(
            barrier, inc=1, device_id=(group, neighbour), device_id_type=pl.DeviceIdType.MESH
        )

    def greet(k):
        pl.semaphore_signal(
            barrier, inc=1, device_id=(peer(k), place), device_id_type=pl.DeviceIdType.MESH
        )

    over_peers(greet)
    pl.semaphore_wait(barrier, group_width + 1)

    for part in travel:
        far_copy(part).start()
    for kind in (TEXT, IMAGE):
        over_peers(lambda k: near_copy(kind, k).start())

    factor, offset = scale[0], shift[0]
    outputs = (grad_images, grad_texts)

    def meet(kind, block, first=False):
        z = lax.dot_general(
            block, own(1 - kind)[...], (((1,), (1,)), ((), ())), preferred_element_type=jnp.float32
        )
        z = factor * z + offset
        if first:
            same = lax.broadcasted_iota(jnp.int32, z.shape, 0) == (
                lax.broadcasted_iota(jnp.int32, z.shape, 1) + group * rows
            )
            z = jnp.where(same, -z, z)
        small = jnp.exp(-jnp.abs(z))
        slopes = factor * (jnp.where(z >= 0, 1.0, small) / (1.0 + small))
        if first:
            slopes = jnp.where(same, -slopes, slopes)
        if kind == TEXT:
            loss = jnp.sum(jnp.maximum(z, 0.0) + jnp.log1p(small), axis=0, keepdims=True)
            row_loss[...] = loss if first else row_loss[...] + loss
        grad = lax.dot_general(
            slopes.astype(jnp.bfloat16), block, (((0,), (0,)), ((), ())),
            preferred_element_type=jnp.float32,
        )
        out = outputs[kind]
        out[...] = grad if first else out[...] + grad

    for kind in (TEXT, IMAGE):
        loads(kind).wait()
        over_peers(lambda k: near_copy(kind, k).wait_recv())
    for kind in (TEXT, IMAGE):
        meet(kind, near[kind], first=True)

    def meet_far(*parts):
        for part in parts:
            over_peers(lambda k: pass_copy(part, k).wait_recv())
        for part in parts:
            meet(part[0], whole_piece(part)[...])

    def pass_on(part):
        far_copy(part).wait_recv()
        over_peers(lambda k: pass_copy(part, k).start())

    for i in range(0, len(travel), 2):
        pass_on(travel[i])
        pass_on(travel[i + 1])
        if i > 0:
            meet_far(travel[i - 2], travel[i - 1])
    meet_far(travel[-2], travel[-1])
    row_loss[...] = row_loss[...] / (SPAN * group_width * rows)

    for part in travel:
        far_copy(part).wait_send()

    def sent(k):
        for kind in (TEXT, IMAGE):
            near_copy(kind, k).wait_send()
        for part in travel:
            pass_copy(part, k).wait_send()

    over_peers(sent)


def store(*refs):
    count = len(refs) // 2
    held, out, sem = refs[:count], refs[count:-1], refs[-1]
    copies = [pltpu.make_async_copy(a, b, sem.at[i]) for i, (a, b) in enumerate(zip(held, out))]
    for copy in copies:
        copy.start()
    for copy in copies:
        copy.wait()


def shards(group_width, cycle, images, texts, scale, shift):
    rows, width = images.shape
    flops = 4 * 2 * rows * SPAN * group_width * rows * width
    shapes = (
        jax.ShapeDtypeStruct((rows, width), jnp.float32),
        jax.ShapeDtypeStruct((rows, width), jnp.float32),
        jax.ShapeDtypeStruct((1, rows), jnp.float32),
    )
    results = pl.pallas_call(
        functools.partial(kernel, group_width, cycle),
        out_shape=shapes,
        in_specs=[pl.BlockSpec(memory_space=pltpu.HBM)] * 2
        + [pl.BlockSpec(memory_space=pltpu.SMEM)] * 2,
        out_specs=[pl.BlockSpec(memory_space=pltpu.VMEM)] * 3,
        scratch_shapes=[
            pltpu.VMEM((2, group_width * rows, width), images.dtype),
            pltpu.VMEM((2, group_width * rows, width), images.dtype),
            pltpu.SemaphoreType.DMA((2,)),
            pltpu.SemaphoreType.DMA((2, group_width)),
            pltpu.SemaphoreType.DMA((2, group_width)),
            pltpu.SemaphoreType.DMA((2, len(EIGHTHS))),
            pltpu.SemaphoreType.DMA((2, len(EIGHTHS))),
            pltpu.SemaphoreType.DMA((2, len(EIGHTHS), group_width)),
            pltpu.SemaphoreType.DMA((2, len(EIGHTHS), group_width)),
        ],
        compiler_params=pltpu.CompilerParams(
            collective_id=0, has_side_effects=True, vmem_limit_bytes=32 << 20
        ),
        cost_estimate=pl.CostEstimate(
            flops=flops, bytes_accessed=16 * rows * width, transcendentals=0
        ),
    )(
        pltpu.with_memory_space_constraint(images, pltpu.HBM),
        pltpu.with_memory_space_constraint(texts, pltpu.HBM),
        scale,
        shift,
    )
    grad_images, grad_texts, row_loss = pl.pallas_call(
        store,
        out_shape=shapes,
        in_specs=[pl.BlockSpec(memory_space=pltpu.VMEM)] * 3,
        out_specs=[pl.BlockSpec(memory_space=pltpu.HBM)] * 3,
        scratch_shapes=[pltpu.SemaphoreType.DMA((3,))],
        compiler_params=pltpu.CompilerParams(vmem_limit_bytes=8 << 20),
        cost_estimate=pl.CostEstimate(
            flops=0, bytes_accessed=16 * rows * width, transcendentals=0
        ),
    )(*results)
    return grad_images, grad_texts, row_loss.reshape(rows)


def solution(mesh):
    placed = (P(("group", "blk"), None), P(("group", "blk"), None), P(), P())
    return jax.shard_map(
        functools.partial(shards, mesh.shape["group"], mesh.shape["blk"]),
        mesh=mesh,
        in_specs=placed,
        out_specs=(P(("group", "blk"), None), P(("group", "blk"), None), P(("group", "blk"))),
        check_vma=False,
    )
```

```python
import functools

import jax
import jax.numpy as jnp
from jax import lax
from jax.experimental import pallas as pl
from jax.experimental.pallas import tpu as pltpu
from jax.sharding import PartitionSpec as P

SPAN = 2
PIECES = 4
TEXT, IMAGE, RELAY = 0, 1, 2


def kernel(
    group_width, cycle, images, texts, scale, shift, grad_images, grad_texts, row_loss,
    near, far, load_sem, near_send, near_recv, far_send, far_recv, pass_send, pass_recv,
):
    group, place = lax.axis_index("group"), lax.axis_index("blk")
    after, before = lax.rem(place + 1, cycle), lax.rem(place + cycle - 1, cycle)
    rows = images.shape[0]
    piece = rows // PIECES
    sources = (texts, images)
    spot = lax.rem(place, 4) if cycle % 4 == 0 else -1
    detour = spot == 2
    onward = (after, jnp.where(detour, after, before))
    slots = (TEXT, jnp.where(detour, RELAY, IMAGE))

    def peer(k):
        return lax.rem(group + k, group_width)

    def over_peers(body):
        if group_width <= 2:
            for k in range(1, group_width):
                body(k)
        else:
            pl.loop(1, group_width)(body)

    def own(kind):
        return near.at[kind, pl.ds(pl.multiple_of(group * rows, rows), rows)]

    def own_piece(kind, c):
        return far.at[kind, c, pl.ds(pl.multiple_of(group * piece, piece), piece)]

    def loads(kind):
        return pltpu.make_async_copy(sources[kind], own(kind), load_sem.at[kind])

    def near_copy(kind, k):
        return pltpu.make_async_remote_copy(
            src_ref=sources[kind], dst_ref=own(kind),
            send_sem=near_send.at[kind, k], recv_sem=near_recv.at[kind, k],
            device_id=(peer(k), place), device_id_type=pl.DeviceIdType.MESH,
        )

    def far_copy(kind, c):
        return pltpu.make_async_remote_copy(
            src_ref=sources[kind].at[pl.ds(c * piece, piece)],
            dst_ref=own_piece(slots[kind], c),
            send_sem=far_send.at[kind, c], recv_sem=far_recv.at[slots[kind], c],
            device_id=(group, onward[kind]), device_id_type=pl.DeviceIdType.MESH,
        )

    def relay_copy(c):
        return pltpu.make_async_remote_copy(
            src_ref=own_piece(RELAY, c), dst_ref=own_piece(IMAGE, c),
            send_sem=far_send.at[RELAY, c], recv_sem=far_recv.at[IMAGE, c],
            device_id=(group, lax.rem(place + cycle - 2, cycle)),
            device_id_type=pl.DeviceIdType.MESH,
        )

    def far_wait(slot, c):
        pltpu.make_async_remote_copy(
            src_ref=own_piece(slot, c), dst_ref=own_piece(slot, c),
            send_sem=far_send.at[slot, c], recv_sem=far_recv.at[slot, c],
            device_id=(group, before), device_id_type=pl.DeviceIdType.MESH,
        ).wait_recv()

    def pass_copy(kind, c, k):
        return pltpu.make_async_remote_copy(
            src_ref=own_piece(kind, c), dst_ref=own_piece(kind, c),
            send_sem=pass_send.at[kind, c, k], recv_sem=pass_recv.at[kind, c, k],
            device_id=(peer(k), place), device_id_type=pl.DeviceIdType.MESH,
        )

    for kind in (TEXT, IMAGE):
        loads(kind).start()
    barrier = pltpu.get_barrier_semaphore()
    for neighbour in (after, before):
        pl.semaphore_signal(
            barrier, inc=1, device_id=(group, neighbour), device_id_type=pl.DeviceIdType.MESH
        )

    def greet(k):
        pl.semaphore_signal(
            barrier, inc=1, device_id=(peer(k), place), device_id_type=pl.DeviceIdType.MESH
        )

    over_peers(greet)

    @pl.when(spot == 1)
    def _():
        pl.semaphore_signal(
            barrier, inc=1, device_id=(group, lax.rem(place + 2, cycle)),
            device_id_type=pl.DeviceIdType.MESH,
        )

    relays = (spot == 3) if cycle % 4 == 0 else False
    pl.semaphore_wait(barrier, group_width + 1 + jnp.where(relays, 1, 0))

    for c in range(PIECES):
        for kind in (TEXT, IMAGE):
            far_copy(kind, c).start()
    for kind in (TEXT, IMAGE):
        over_peers(lambda k: near_copy(kind, k).start())

    factor, offset = scale[0], shift[0]
    outputs = (grad_images, grad_texts)

    def meet(kind, block, first=False):
        z = lax.dot_general(
            block, own(1 - kind)[...], (((1,), (1,)), ((), ())), preferred_element_type=jnp.float32
        )
        z = factor * z + offset
        if first:
            same = lax.broadcasted_iota(jnp.int32, z.shape, 0) == (
                lax.broadcasted_iota(jnp.int32, z.shape, 1) + group * rows
            )
            z = jnp.where(same, -z, z)
        small = jnp.exp(-jnp.abs(z))
        slopes = factor * (jnp.where(z >= 0, 1.0, small) / (1.0 + small))
        if first:
            slopes = jnp.where(same, -slopes, slopes)
        if kind == TEXT:
            loss = jnp.sum(jnp.maximum(z, 0.0) + jnp.log1p(small), axis=0, keepdims=True)
            row_loss[...] = loss if first else row_loss[...] + loss
        grad = lax.dot_general(
            slopes.astype(jnp.bfloat16), block, (((0,), (0,)), ((), ())),
            preferred_element_type=jnp.float32,
        )
        out = outputs[kind]
        out[...] = grad if first else out[...] + grad

    for kind in (TEXT, IMAGE):
        loads(kind).wait()
        over_peers(lambda k: near_copy(kind, k).wait_recv())
    for kind in (TEXT, IMAGE):
        meet(kind, near[kind], first=True)

    def meet_far(c):
        for kind in (TEXT, IMAGE):
            over_peers(lambda k: pass_copy(kind, c, k).wait_recv())
        for kind in (TEXT, IMAGE):
            meet(kind, far[kind, c])

    for c in range(PIECES):

        @pl.when(spot == 3)
        def _():
            far_wait(RELAY, c)
            relay_copy(c).start()

        for kind in (TEXT, IMAGE):
            far_wait(kind, c)
            over_peers(lambda k: pass_copy(kind, c, k).start())
        if c > 0:
            meet_far(c - 1)
    meet_far(PIECES - 1)
    row_loss[...] = row_loss[...] / (SPAN * group_width * rows)

    for kind in (TEXT, IMAGE):
        for c in range(PIECES):
            far_copy(kind, c).wait_send()

    @pl.when(spot == 3)
    def _():
        for c in range(PIECES):
            relay_copy(c).wait_send()

    def sent(k):
        for kind in (TEXT, IMAGE):
            near_copy(kind, k).wait_send()
            for c in range(PIECES):
                pass_copy(kind, c, k).wait_send()

    over_peers(sent)


def store(*refs):
    count = len(refs) // 2
    held, out, sem = refs[:count], refs[count:-1], refs[-1]
    copies = [pltpu.make_async_copy(a, b, sem.at[i]) for i, (a, b) in enumerate(zip(held, out))]
    for copy in copies:
        copy.start()
    for copy in copies:
        copy.wait()


def shards(group_width, cycle, images, texts, scale, shift):
    rows, width = images.shape
    flops = 4 * 2 * rows * SPAN * group_width * rows * width
    shapes = (
        jax.ShapeDtypeStruct((rows, width), jnp.float32),
        jax.ShapeDtypeStruct((rows, width), jnp.float32),
        jax.ShapeDtypeStruct((1, rows), jnp.float32),
    )
    results = pl.pallas_call(
        functools.partial(kernel, group_width, cycle),
        out_shape=shapes,
        in_specs=[pl.BlockSpec(memory_space=pltpu.HBM)] * 2
        + [pl.BlockSpec(memory_space=pltpu.SMEM)] * 2,
        out_specs=[pl.BlockSpec(memory_space=pltpu.VMEM)] * 3,
        scratch_shapes=[
            pltpu.VMEM((2, group_width * rows, width), images.dtype),
            pltpu.VMEM((3, PIECES, group_width * rows // PIECES, width), images.dtype),
            pltpu.SemaphoreType.DMA((2,)),
            pltpu.SemaphoreType.DMA((2, group_width)),
            pltpu.SemaphoreType.DMA((2, group_width)),
            pltpu.SemaphoreType.DMA((3, PIECES)),
            pltpu.SemaphoreType.DMA((3, PIECES)),
            pltpu.SemaphoreType.DMA((2, PIECES, group_width)),
            pltpu.SemaphoreType.DMA((2, PIECES, group_width)),
        ],
        compiler_params=pltpu.CompilerParams(
            collective_id=0, has_side_effects=True, vmem_limit_bytes=32 << 20
        ),
        cost_estimate=pl.CostEstimate(
            flops=flops, bytes_accessed=16 * rows * width, transcendentals=0
        ),
    )(
        pltpu.with_memory_space_constraint(images, pltpu.HBM),
        pltpu.with_memory_space_constraint(texts, pltpu.HBM),
        scale,
        shift,
    )
    grad_images, grad_texts, row_loss = pl.pallas_call(
        store,
        out_shape=shapes,
        in_specs=[pl.BlockSpec(memory_space=pltpu.VMEM)] * 3,
        out_specs=[pl.BlockSpec(memory_space=pltpu.HBM)] * 3,
        scratch_shapes=[pltpu.SemaphoreType.DMA((3,))],
        compiler_params=pltpu.CompilerParams(vmem_limit_bytes=8 << 20),
        cost_estimate=pl.CostEstimate(
            flops=0, bytes_accessed=16 * rows * width, transcendentals=0
        ),
    )(*results)
    return grad_images, grad_texts, row_loss.reshape(rows)


def solution(mesh):
    placed = (P(("group", "blk"), None), P(("group", "blk"), None), P(), P())
    return jax.shard_map(
        functools.partial(shards, mesh.shape["group"], mesh.shape["blk"]),
        mesh=mesh,
        in_specs=placed,
        out_specs=(P(("group", "blk"), None), P(("group", "blk"), None), P(("group", "blk"))),
        check_vma=False,
    )
```

```python
import functools

import jax
import jax.numpy as jnp
from jax import lax
from jax.experimental import pallas as pl
from jax.experimental.pallas import tpu as pltpu
from jax.sharding import PartitionSpec as P

SPAN = 2
PIECES = 2
TEXT, IMAGE = 0, 1


def kernel(
    group_width, cycle, images, texts, scale, shift, grad_images, grad_texts, row_loss,
    near, far, load_sem, near_send, near_recv, far_send, far_recv, pass_send, pass_recv,
):
    group, place = lax.axis_index("group"), lax.axis_index("blk")
    after, before = lax.rem(place + 1, cycle), lax.rem(place + cycle - 1, cycle)
    rows = images.shape[0]
    piece = rows // PIECES
    sources = (texts, images)
    onward = (after, before)

    def peer(k):
        return lax.rem(group + k, group_width)

    def over_peers(body):
        if group_width <= 2:
            for k in range(1, group_width):
                body(k)
        else:
            pl.loop(1, group_width)(body)

    def own(kind):
        return near.at[kind, pl.ds(pl.multiple_of(group * rows, rows), rows)]

    def own_piece(kind, c):
        return far.at[kind, c, pl.ds(pl.multiple_of(group * piece, piece), piece)]

    def loads(kind):
        return pltpu.make_async_copy(sources[kind], own(kind), load_sem.at[kind])

    def near_copy(kind, k):
        return pltpu.make_async_remote_copy(
            src_ref=sources[kind], dst_ref=own(kind),
            send_sem=near_send.at[kind, k], recv_sem=near_recv.at[kind, k],
            device_id=(peer(k), place), device_id_type=pl.DeviceIdType.MESH,
        )

    def far_copy(kind, c):
        return pltpu.make_async_remote_copy(
            src_ref=sources[kind].at[pl.ds(c * piece, piece)], dst_ref=own_piece(kind, c),
            send_sem=far_send.at[kind, c], recv_sem=far_recv.at[kind, c],
            device_id=(group, onward[kind]), device_id_type=pl.DeviceIdType.MESH,
        )

    def pass_copy(kind, c, k):
        return pltpu.make_async_remote_copy(
            src_ref=own_piece(kind, c), dst_ref=own_piece(kind, c),
            send_sem=pass_send.at[kind, c, k], recv_sem=pass_recv.at[kind, c, k],
            device_id=(peer(k), place), device_id_type=pl.DeviceIdType.MESH,
        )

    for kind in (TEXT, IMAGE):
        loads(kind).start()
    barrier = pltpu.get_barrier_semaphore()
    for neighbour in (after, before):
        pl.semaphore_signal(
            barrier, inc=1, device_id=(group, neighbour), device_id_type=pl.DeviceIdType.MESH
        )

    def greet(k):
        pl.semaphore_signal(
            barrier, inc=1, device_id=(peer(k), place), device_id_type=pl.DeviceIdType.MESH
        )

    over_peers(greet)
    pl.semaphore_wait(barrier, group_width + 1)

    for c in range(PIECES):
        for kind in (TEXT, IMAGE):
            far_copy(kind, c).start()
    for kind in (TEXT, IMAGE):
        over_peers(lambda k: near_copy(kind, k).start())

    factor, offset = scale[0], shift[0]
    outputs = (grad_images, grad_texts)

    def meet(kind, block, first=False):
        z = lax.dot_general(
            block, own(1 - kind)[...], (((1,), (1,)), ((), ())), preferred_element_type=jnp.float32
        )
        z = factor * z + offset
        if first:
            same = lax.broadcasted_iota(jnp.int32, z.shape, 0) == (
                lax.broadcasted_iota(jnp.int32, z.shape, 1) + group * rows
            )
            z = jnp.where(same, -z, z)
        small = jnp.exp(-jnp.abs(z))
        slopes = factor * (jnp.where(z >= 0, 1.0, small) / (1.0 + small))
        if first:
            slopes = jnp.where(same, -slopes, slopes)
        if kind == TEXT:
            loss = jnp.sum(jnp.maximum(z, 0.0) + jnp.log1p(small), axis=0, keepdims=True)
            row_loss[...] = loss if first else row_loss[...] + loss
        grad = lax.dot_general(
            slopes.astype(jnp.bfloat16), block, (((0,), (0,)), ((), ())),
            preferred_element_type=jnp.float32,
        )
        out = outputs[kind]
        out[...] = grad if first else out[...] + grad

    for kind in (TEXT, IMAGE):
        loads(kind).wait()
        over_peers(lambda k: near_copy(kind, k).wait_recv())
    for kind in (TEXT, IMAGE):
        meet(kind, near[kind], first=True)

    def meet_far(c):
        for kind in (TEXT, IMAGE):
            over_peers(lambda k: pass_copy(kind, c, k).wait_recv())
        for kind in (TEXT, IMAGE):
            meet(kind, far[kind, c])

    for c in range(PIECES):
        for kind in (TEXT, IMAGE):
            far_copy(kind, c).wait_recv()
            over_peers(lambda k: pass_copy(kind, c, k).start())
        if c > 0:
            meet_far(c - 1)
    meet_far(PIECES - 1)
    row_loss[...] = row_loss[...] / (SPAN * group_width * rows)

    for kind in (TEXT, IMAGE):
        for c in range(PIECES):
            far_copy(kind, c).wait_send()

    def sent(k):
        for kind in (TEXT, IMAGE):
            near_copy(kind, k).wait_send()
            for c in range(PIECES):
                pass_copy(kind, c, k).wait_send()

    over_peers(sent)


def store(*refs):
    count = len(refs) // 2
    held, out, sem = refs[:count], refs[count:-1], refs[-1]
    copies = [pltpu.make_async_copy(a, b, sem.at[i]) for i, (a, b) in enumerate(zip(held, out))]
    for copy in copies:
        copy.start()
    for copy in copies:
        copy.wait()


def shards(group_width, cycle, images, texts, scale, shift):
    rows, width = images.shape
    flops = 4 * 2 * rows * SPAN * group_width * rows * width
    shapes = (
        jax.ShapeDtypeStruct((rows, width), jnp.float32),
        jax.ShapeDtypeStruct((rows, width), jnp.float32),
        jax.ShapeDtypeStruct((1, rows), jnp.float32),
    )
    results = pl.pallas_call(
        functools.partial(kernel, group_width, cycle),
        out_shape=shapes,
        in_specs=[pl.BlockSpec(memory_space=pltpu.HBM)] * 2
        + [pl.BlockSpec(memory_space=pltpu.SMEM)] * 2,
        out_specs=[pl.BlockSpec(memory_space=pltpu.VMEM)] * 3,
        scratch_shapes=[
            pltpu.VMEM((2, group_width * rows, width), images.dtype),
            pltpu.VMEM((2, PIECES, group_width * rows // PIECES, width), images.dtype),
            pltpu.SemaphoreType.DMA((2,)),
            pltpu.SemaphoreType.DMA((2, group_width)),
            pltpu.SemaphoreType.DMA((2, group_width)),
            pltpu.SemaphoreType.DMA((2, PIECES)),
            pltpu.SemaphoreType.DMA((2, PIECES)),
            pltpu.SemaphoreType.DMA((2, PIECES, group_width)),
            pltpu.SemaphoreType.DMA((2, PIECES, group_width)),
        ],
        compiler_params=pltpu.CompilerParams(
            collective_id=0, has_side_effects=True, vmem_limit_bytes=32 << 20
        ),
        cost_estimate=pl.CostEstimate(
            flops=flops, bytes_accessed=16 * rows * width, transcendentals=0
        ),
    )(
        pltpu.with_memory_space_constraint(images, pltpu.HBM),
        pltpu.with_memory_space_constraint(texts, pltpu.HBM),
        scale,
        shift,
    )
    grad_images, grad_texts, row_loss = pl.pallas_call(
        store,
        out_shape=shapes,
        in_specs=[pl.BlockSpec(memory_space=pltpu.VMEM)] * 3,
        out_specs=[pl.BlockSpec(memory_space=pltpu.HBM)] * 3,
        scratch_shapes=[pltpu.SemaphoreType.DMA((3,))],
        compiler_params=pltpu.CompilerParams(vmem_limit_bytes=8 << 20),
        cost_estimate=pl.CostEstimate(
            flops=0, bytes_accessed=16 * rows * width, transcendentals=0
        ),
    )(*results)
    return grad_images, grad_texts, row_loss.reshape(rows)


def solution(mesh):
    placed = (P(("group", "blk"), None), P(("group", "blk"), None), P(), P())
    return jax.shard_map(
        functools.partial(shards, mesh.shape["group"], mesh.shape["blk"]),
        mesh=mesh,
        in_specs=placed,
        out_specs=(P(("group", "blk"), None), P(("group", "blk"), None), P(("group", "blk"))),
        check_vma=False,
    )
```
